32 devices in a mesh: dom: 8 (over z, core), st: 4 (over y, x).
Axes of the slice: x: 2, y: 2, z: 4, core: 2. Of those that a mesh axis runs over, the one named last changes fastest.
Arguments:
- orbitals: bfloat16 [384, 16384], P('st', 'dom')
- cell_matrix: bfloat16 [512, 512], replicated
- connectivity: int32 [128, 512], P('dom'), may hold values from 0 to 2303, as said below
- surface_nodes: int32 [8, 256], P('dom'), may hold values from 0 to 2047, as said below
- cell_scale: float32 [128], P('dom'), may hold values from 0.3 to 3
- potential: float32 [16384], P('dom'), may hold values from -1 to 2
Outputs:
- rotated_states: bfloat16 [384, 16384], P('st', 'dom')
The draws below stay inside these ranges and needn't reach their ends.
Inputs may be any that keep to these rules, and one draw needn't show every extreme that they name: `connectivity`: within a cell all 512 numbers differ. In each domain the first 12 cells name only the domain's own nodes (numbers below 2048); the others may also name the 256 shared-surface nodes of the next domain. `surface_nodes`: each row names 256 different nodes.
All inputs are finite; a program needn't handle non-finite values.
Results may differ from the reference program's by a relative error of at most 0.002.
The reference program's roundings to bfloat16 on the way count: a program that leaves them out, or rounds other values in their place, can miss the bound.
Values may be sent and summed in bfloat16 or wider, within the bound.
A program may use at most 64 MiB of HBM per device.

```python
import math
import jax
import jax.numpy as jnp
from jax import lax

NODE_CELL = 512
STATES = 384
NODES_DEV = 2048
CELLS_DEV = 16
DEGREE = 3
ROOT_ITERS = 4
SURF = 256
DOMAINS = 8
NODES = 16384
CELLS = 128
N_DOM = 8


def draw_orbitals(key, part):
    key_values, key_scales = jax.random.split(key)
    key_domain = jax.random.fold_in(key, 7)
    key_heavy = jax.random.fold_in(key, 11)
    values = jnp.clip(jax.random.normal(key_values, (STATES, NODES), jnp.float32), -6.0, 6.0)
    scales = jnp.exp(jax.random.uniform(key_scales, (STATES, 1), jnp.float32, 0.0, math.log(3.0)))
    domain_amp = jnp.exp(jax.random.uniform(key_domain, (DOMAINS,), jnp.float32, 0.0, math.log(4.0)))
    heavy = jax.random.randint(key_heavy, (), 0, DOMAINS, dtype=jnp.int32)
    domain_ids = jnp.arange(DOMAINS, dtype=jnp.int32)
    domain_amp = jnp.where(domain_ids == heavy, 4.0, domain_amp)
    node_amp = jnp.repeat(domain_amp, NODES_DEV)[None, :]
    return (values * scales * node_amp).astype(jnp.bfloat16)


def draw_cell_matrix(key, part):
    base = jax.random.normal(key, (NODE_CELL, NODE_CELL), jnp.float32)
    base = base * (0.7 / math.sqrt(NODE_CELL))
    row_ids = lax.broadcasted_iota(jnp.int32, (NODE_CELL, NODE_CELL), 0)
    col_ids = lax.broadcasted_iota(jnp.int32, (NODE_CELL, NODE_CELL), 1)
    diagonal = jnp.where(row_ids == col_ids, 2.0, 0.0)
    return (0.5 * (base + base.T) + diagonal).astype(jnp.bfloat16)


def draw_connectivity(key, part):
    width_all = NODES_DEV + SURF
    col_ids = jnp.arange(width_all, dtype=jnp.int32)[None, :]
    cell_ids = jnp.arange(CELLS, dtype=jnp.int32)[:, None]
    scores = jax.random.randint(key, (CELLS, width_all), 0, 65536, dtype=jnp.int32) * 8192 + col_ids
    inner = cell_ids % CELLS_DEV < CELLS_DEV - CELLS_DEV // 4
    is_ghost = col_ids >= NODES_DEV
    scores = jnp.where(inner & is_ghost, scores + 1073741824, scores)
    forced = (cell_ids == CELLS_DEV - 1) & ((col_ids == 0) | (col_ids == width_all - 1))
    scores = jnp.where(forced, -1, scores)
    order = jnp.argsort(scores, axis=1, stable=True)
    return order[:, :NODE_CELL].astype(jnp.int32)


def draw_surface_nodes(key, part):
    col_ids = jnp.arange(NODES_DEV, dtype=jnp.int32)[None, :]
    row_ids = jnp.arange(DOMAINS, dtype=jnp.int32)[:, None]
    scores = jax.random.randint(key, (DOMAINS, NODES_DEV), 0, 65536, dtype=jnp.int32) * 8192 + col_ids
    forced = (row_ids == 0) & ((col_ids == 0) | (col_ids == NODES_DEV - 1))
    scores = jnp.where(forced, -1, scores)
    order = jnp.argsort(scores, axis=1, stable=True)
    return order[:, :SURF].astype(jnp.int32)


def levels(rng, extent, pieces, least, high):
    loudness = 1.0
    for dim, shards_of in pieces:
        draws = jax.random.uniform(jax.random.fold_in(jax.random.fold_in(rng, 6), dim), (shards_of,), jnp.float32, least / len(pieces), high / len(pieces))
        loudness = loudness * jnp.repeat(jnp.exp(draws), extent[dim] // shards_of).reshape((-1,) + (1,) * (len(extent) - 1 - dim))
    return loudness


def setup_inputs(seed: int = 0) -> dict:
    streams_of = jax.random.split(jax.random.key(seed), 7)
    return {
        "orbitals": draw_orbitals(jax.random.fold_in(streams_of[6], 71), 0),
        "cell_matrix": draw_cell_matrix(jax.random.fold_in(streams_of[6], 71), 0),
        "connectivity": draw_connectivity(jax.random.fold_in(streams_of[6], 71), 0),
        "surface_nodes": draw_surface_nodes(jax.random.fold_in(streams_of[6], 71), 0),
        "cell_scale": jnp.clip(jnp.exp(math.log(3.0) - 2.3025851 * jax.random.uniform(streams_of[4], (CELLS,), jnp.float32) ** levels(streams_of[4], (CELLS,), ((0, 8),), -0.2, 0.2)), 0.3, 3.0),
        "potential": jnp.clip(-1.0 + 3.0 * jax.random.uniform(streams_of[5], (NODES,), jnp.float32) ** levels(streams_of[5], (NODES,), ((0, 8),), -0.2, 0.2), -1.0, 2.0),
    }


center = 7.0
half_width = 6.0
epsilon = 1e-06

def apply_hamiltonian(values, global_conn, cell_scale, potential, cell_matrix):
    padded = jnp.concatenate([values, jnp.zeros((values.shape[0], 1), values.dtype)], axis=1)
    totals = jnp.zeros(padded.shape, jnp.float32)

    def one_domain(domain, totals):
        indices = global_conn[domain]
        gathered = padded[:, indices]
        products = jnp.dot(gathered.reshape(-1, NODE_CELL), cell_matrix, preferred_element_type=jnp.float32)
        scales = lax.dynamic_slice_in_dim(cell_scale, domain * CELLS_DEV, CELLS_DEV)
        products = products.reshape(values.shape[0], CELLS_DEV, NODE_CELL) * scales[None, :, None]
        return totals.at[:, indices].add(products)
    totals = lax.fori_loop(0, N_DOM, one_domain, totals)
    return totals[:, :NODES] + potential[None, :] * values.astype(jnp.float32)

def newton_root(gram):
    highest = lax.Precision.HIGHEST
    scale_sum = jnp.sqrt(jnp.sum(gram * gram)) + epsilon
    identity = jnp.eye(STATES, dtype=jnp.float32)
    growing = gram / scale_sum
    inverse = identity
    for iteration in range(ROOT_ITERS):
        factor = 1.5 * identity - 0.5 * jnp.dot(inverse, growing, precision=highest)
        growing = jnp.dot(growing, factor, precision=highest)
        inverse = jnp.dot(factor, inverse, precision=highest)
    return (inverse, scale_sum)

def reference(orbitals, cell_matrix, connectivity, surface_nodes, cell_scale, potential):
    domains = jnp.arange(N_DOM, dtype=jnp.int32)
    upper_ids = jnp.roll(surface_nodes, -1, axis=0) + (domains[:, None] + 1) * NODES_DEV
    upper_ids = jnp.where(domains[:, None] == N_DOM - 1, NODES, upper_ids)
    own_nodes = domains[:, None] * NODES_DEV + jnp.arange(NODES_DEV, dtype=jnp.int32)[None, :]
    ext_map = jnp.concatenate([own_nodes, upper_ids], axis=1).astype(jnp.int32)
    local_conn = connectivity.reshape(N_DOM, CELLS_DEV * NODE_CELL).astype(jnp.int32)
    global_conn = jnp.take_along_axis(ext_map, local_conn, axis=1).reshape(N_DOM, CELLS_DEV, NODE_CELL)
    older = orbitals
    newest = orbitals
    for degree_step in range(DEGREE):
        image = apply_hamiltonian(newest, global_conn, cell_scale, potential, cell_matrix)
        shifted = (image - center * newest.astype(jnp.float32)) / half_width
        if degree_step == 0:
            fresh = shifted
        else:
            fresh = 2.0 * shifted - older.astype(jnp.float32)
        older = newest
        newest = fresh.astype(jnp.bfloat16)
    gram = jnp.dot(newest, newest.T, preferred_element_type=jnp.float32)
    inverse, scale_sum = newton_root(gram)
    rotation = (inverse * jnp.sqrt(NODES / scale_sum)).astype(jnp.bfloat16)
    return jnp.dot(rotation.T, newest, preferred_element_type=jnp.float32).astype(jnp.bfloat16)
```

```python
import functools

import jax
import jax.numpy as jnp
from jax import lax
from jax.experimental import pallas as pl
from jax.experimental.pallas import tpu as pltpu
from jax.sharding import PartitionSpec as P

DEGREE = 3
ROOT_ITERS = 4
MESH = pl.DeviceIdType.MESH

center = 7.0
half_width = 6.0
epsilon = 1e-06

NT = (((1,), (1,)), ((), ()))


def halves(values):
    high = values.astype(jnp.bfloat16)
    low = (values - high.astype(jnp.float32)).astype(jnp.bfloat16)
    return jnp.concatenate([high, low], axis=0)


def filter_kernel(
    n_dom, inner,
    f_ref, matrix_ref, conn_ref, surface_ref, scale_ref, potential_ref, out_ref,
    extended, middle, totals, picks, surface_pick, pair, edge_out, edge_in, back_out, back_in,
    edge_send, edge_recv, back_send, back_recv,
):
    states, nodes = f_ref.shape
    surf = surface_ref.shape[1]
    cells = conn_ref.shape[0]
    width = nodes + surf
    tile = 256
    me = lax.axis_index("dom")
    after, before = lax.rem(me + 1, n_dom), lax.rem(me + n_dom - 1, n_dom)

    barrier = pltpu.get_barrier_semaphore()
    for neighbour in (after, before):
        pl.semaphore_signal(barrier, inc=1, device_id={"dom": neighbour}, device_id_type=MESH)

    def one_hot(ids, start, rows):
        node = start + lax.broadcasted_iota(jnp.int32, (rows, ids.shape[1]), 0)
        return jnp.where(node == ids, 1.0, 0.0).astype(jnp.bfloat16)

    for start in range(0, nodes, tile):
        surface_pick[pl.ds(start, tile), :] = one_hot(surface_ref[...], start, tile)

    def add_back(parts, pick, start, rows):
        spread = lax.dot_general(parts, pick, NT, preferred_element_type=jnp.float32)
        totals[:, pl.ds(start, rows)] += spread[:states] + spread[states:]

    def run_cells(first, last, extent, build):
        def one_cell(cell, carry):
            if build:
                ids = conn_ref[pl.ds(cell, 1), :]
                for start in range(0, extent, tile):
                    picks[cell, pl.ds(start, tile), :] = one_hot(ids, start, tile)
            gathered = jnp.dot(
                extended[:, :extent], picks[cell, :extent, :], preferred_element_type=jnp.float32
            ).astype(jnp.bfloat16)
            products = jnp.dot(gathered, matrix_ref[...], preferred_element_type=jnp.float32)
            pair[...] = halves(products * scale_ref[cell])
            for start in range(0, extent, tile):
                add_back(pair[...], picks[cell, pl.ds(start, tile), :], start, tile)
            return carry

        lax.fori_loop(first, last, one_cell, 0)

    extended[:, :nodes] = f_ref[...]
    for step in range(DEGREE):
        edge_out[step] = jnp.dot(
            extended[:, :nodes], surface_pick[...], preferred_element_type=jnp.float32
        ).astype(jnp.bfloat16)
        if step == 0:
            pl.semaphore_wait(barrier, 2)
        edge = pltpu.make_async_remote_copy(
            src_ref=edge_out.at[step], dst_ref=edge_in.at[step],
            send_sem=edge_send.at[step], recv_sem=edge_recv.at[step],
            device_id={"dom": before}, device_id_type=MESH,
        )
        edge.start()
        totals[...] = jnp.zeros_like(totals)
        run_cells(0, inner // 2, nodes, step == 0)
        edge.wait()
        ghosts = edge_in[step]
        extended[:, nodes:] = jnp.where(me == n_dom - 1, jnp.zeros_like(ghosts), ghosts)
        run_cells(inner, cells, width, step == 0)
        back_out[step] = totals[:, nodes:]
        back = pltpu.make_async_remote_copy(
            src_ref=back_out.at[step], dst_ref=back_in.at[step],
            send_sem=back_send.at[step], recv_sem=back_recv.at[step],
            device_id={"dom": after}, device_id_type=MESH,
        )
        back.start()
        run_cells(inner // 2, inner, nodes, step == 0)
        back.wait()
        returned = back_in[step]
        returned = jnp.where(me == 0, jnp.zeros_like(returned), returned)
        parts = halves(returned)
        for start in range(0, nodes, tile):
            add_back(parts, surface_pick[pl.ds(start, tile), :], start, tile)
        for start in range(0, nodes, tile):
            columns = pl.ds(start, tile)
            newest = extended[:, columns].astype(jnp.float32)
            image = totals[:, columns] + potential_ref[:, columns] * newest
            fresh = (image - center * newest) / half_width
            if step > 0:
                older = f_ref if step == 1 else middle
                fresh = 2.0 * fresh - older[:, columns].astype(jnp.float32)
            fresh = fresh.astype(jnp.bfloat16)
            if step == DEGREE - 1:
                out_ref[:, columns] = fresh
            else:
                extended[:, columns] = fresh
                if step == 0:
                    middle[:, columns] = fresh


def filtered_states(orbitals, cell_matrix, connectivity, surface_nodes, cell_scale, potential):
    states, nodes = orbitals.shape
    cells, node_cell = connectivity.shape
    surf = surface_nodes.shape[1]
    vmem = pl.BlockSpec(memory_space=pltpu.VMEM)
    smem = pl.BlockSpec(memory_space=pltpu.SMEM)
    bf16, f32 = jnp.bfloat16, jnp.float32
    return pl.pallas_call(
        functools.partial(filter_kernel, lax.axis_size("dom"), cells - cells // 4),
        out_shape=jax.ShapeDtypeStruct((states, nodes), bf16),
        in_specs=[vmem, vmem, vmem, vmem, smem, vmem],
        out_specs=vmem,
        scratch_shapes=[
            pltpu.VMEM((states, nodes + surf), bf16),
            pltpu.VMEM((states, nodes), bf16),
            pltpu.VMEM((states, nodes + surf), f32),
            pltpu.VMEM((cells, nodes + surf, node_cell), bf16),
            pltpu.VMEM((nodes, surf), bf16),
            pltpu.VMEM((2 * states, node_cell), bf16),
            pltpu.VMEM((DEGREE, states, surf), bf16),
            pltpu.VMEM((DEGREE, states, surf), bf16),
            pltpu.VMEM((DEGREE, states, surf), f32),
            pltpu.VMEM((DEGREE, states, surf), f32),
        ] + [pltpu.SemaphoreType.DMA((DEGREE,))] * 4,
        compiler_params=pltpu.CompilerParams(
            collective_id=0, has_side_effects=True, vmem_limit_bytes=52 * 1024 * 1024
        ),
        name="chebyshev_filter",
    )(orbitals, cell_matrix, connectivity, surface_nodes, cell_scale, potential[None, :])


def newton_root(gram):
    highest = lax.Precision.HIGHEST
    states_all = gram.shape[0]
    scale_sum = jnp.sqrt(jnp.sum(gram * gram)) + epsilon
    identity = jnp.eye(states_all, dtype=jnp.float32)
    growing = gram / scale_sum
    inverse = identity
    for iteration in range(ROOT_ITERS):
        factor = 1.5 * identity - 0.5 * jnp.dot(inverse, growing, precision=highest)
        growing = jnp.dot(growing, factor, precision=highest)
        inverse = jnp.dot(factor, inverse, precision=highest)
    return (inverse, scale_sum)


def body(orbitals, cell_matrix, connectivity, surface_nodes, cell_scale, potential):
    newest = filtered_states(
        orbitals, cell_matrix, connectivity, surface_nodes, cell_scale, potential
    )
    slabs = lax.all_to_all(newest, "st", split_axis=1, concat_axis=0, tiled=True)
    gram_part = jnp.dot(slabs, slabs.T, preferred_element_type=jnp.float32)
    row_block = lax.psum_scatter(gram_part, "st", scatter_dimension=0, tiled=True)
    row_block = lax.psum(row_block, "dom")
    gram = lax.all_gather(row_block, "st", axis=0, tiled=True)
    inverse, scale_sum = newton_root(gram)
    node_total = lax.axis_size("dom") * orbitals.shape[1]
    rotation = (inverse * jnp.sqrt(node_total / scale_sum)).astype(jnp.bfloat16)
    rotated = jnp.dot(rotation.T, slabs, preferred_element_type=jnp.float32).astype(jnp.bfloat16)
    return lax.all_to_all(rotated, "st", split_axis=0, concat_axis=1, tiled=True)


def solution(mesh):
    return jax.shard_map(
        body,
        mesh=mesh,
        in_specs=(P("st", "dom"), P(), P("dom", None), P("dom", None), P("dom"), P("dom")),
        out_specs=P("st", "dom"),
        check_vma=False,
    )
```

```python
import functools

import jax
import jax.numpy as jnp
from jax import lax
from jax.experimental import pallas as pl
from jax.experimental.pallas import tpu as pltpu
from jax.sharding import PartitionSpec as P

DEGREE = 3
ROOT_ITERS = 4
MESH = pl.DeviceIdType.MESH

center = 7.0
half_width = 6.0
epsilon = 1e-06

NT = (((1,), (1,)), ((), ()))


def halves(values):
    high = values.astype(jnp.bfloat16)
    low = (values - high.astype(jnp.float32)).astype(jnp.bfloat16)
    return jnp.concatenate([high, low], axis=0)


def filter_kernel(
    n_dom, inner,
    f_ref, matrix_ref, conn_ref, surface_ref, scale_ref, potential_ref, out_ref,
    extended, history, totals, picks, surface_pick, pair, edge_out, edge_in, back_out, back_in,
    edge_send, edge_recv, back_send, back_recv,
):
    states, nodes = f_ref.shape
    surf = surface_ref.shape[1]
    cells, node_cell = conn_ref.shape
    width = nodes + surf
    tile = 256
    me = lax.axis_index("dom")
    after, before = lax.rem(me + 1, n_dom), lax.rem(me + n_dom - 1, n_dom)

    barrier = pltpu.get_barrier_semaphore()
    for neighbour in (after, before):
        pl.semaphore_signal(barrier, inc=1, device_id={"dom": neighbour}, device_id_type=MESH)

    def one_hot(ids, start):
        columns = ids.shape[1]
        node = lax.broadcasted_iota(jnp.int32, (tile, columns), 0).astype(jnp.bfloat16)
        wanted = jnp.broadcast_to((ids - start).astype(jnp.bfloat16), (tile, columns))
        one, zero = jnp.bfloat16(1), jnp.bfloat16(0)
        return jnp.where(node == wanted, one, zero)

    for start in range(0, nodes, tile):
        surface_pick[pl.ds(start, tile), :] = one_hot(surface_ref[...], start)
    for cell in range(cells):
        ids = conn_ref[pl.ds(cell, 1), :]
        lanes = pl.ds(cell * node_cell, node_cell)

        def build_tile(index, carry):
            start = index * tile
            picks[pl.ds(pl.multiple_of(start, tile), tile), lanes] = one_hot(ids, start)
            return carry

        lax.fori_loop(0, (nodes if cell < inner else width) // tile, build_tile, 0)

    def run_cells(first, last, extent):
        count = last - first
        gathered = []
        for cell in range(first, last):
            lanes = pl.ds(cell * node_cell, node_cell)
            gathered.append(jnp.dot(
                extended[:, :extent], picks[:extent, lanes], preferred_element_type=jnp.float32
            ).astype(jnp.bfloat16))
        products = jnp.dot(
            jnp.concatenate(gathered, axis=0), matrix_ref[...], preferred_element_type=jnp.float32
        )
        for index in range(count):
            scaled = products[index * states:(index + 1) * states] * scale_ref[first + index]
            pair[:, index * node_cell:(index + 1) * node_cell] = halves(scaled)
        group = pl.ds(first * node_cell, count * node_cell)

        def scatter_tile(index, carry):
            rows = pl.ds(pl.multiple_of(index * tile, tile), tile)
            spread = lax.dot_general(
                pair[:, :count * node_cell], picks[rows, group], NT,
                preferred_element_type=jnp.float32,
            )
            totals[:, rows] += spread[:states] + spread[states:]
            return carry

        lax.fori_loop(0, extent // tile, scatter_tile, 0)

    extended[:, :nodes] = f_ref[...]
    pl.semaphore_wait(barrier, 2)

    def one_step(step, carry):
        edge_out[step] = jnp.dot(
            extended[:, :nodes], surface_pick[...], preferred_element_type=jnp.float32
        ).astype(jnp.bfloat16)
        edge = pltpu.make_async_remote_copy(
            src_ref=edge_out.at[step], dst_ref=edge_in.at[step],
            send_sem=edge_send.at[step], recv_sem=edge_recv.at[step],
            device_id={"dom": before}, device_id_type=MESH,
        )
        edge.start()
        totals[...] = jnp.zeros_like(totals)
        run_cells(0, inner // 2, nodes)
        edge.wait()
        ghosts = edge_in[step]
        extended[:, nodes:] = jnp.where(me == n_dom - 1, jnp.zeros_like(ghosts), ghosts)
        run_cells(inner, cells, width)
        back_out[step] = totals[:, nodes:]
        back = pltpu.make_async_remote_copy(
            src_ref=back_out.at[step], dst_ref=back_in.at[step],
            send_sem=back_send.at[step], recv_sem=back_recv.at[step],
            device_id={"dom": after}, device_id_type=MESH,
        )
        back.start()
        run_cells(inner // 2, inner, nodes)
        back.wait()
        returned = back_in[step]
        returned = jnp.where(me == 0, jnp.zeros_like(returned), returned)
        parts = halves(returned)
        first = step == 0
        for start in range(0, nodes, tile):
            columns = pl.ds(start, tile)
            spread = lax.dot_general(
                parts, surface_pick[columns, :], NT, preferred_element_type=jnp.float32
            )
            total = totals[:, columns] + (spread[:states] + spread[states:])
            old = extended[:, columns]
            newest = old.astype(jnp.float32)
            image = total + potential_ref[:, columns] * newest
            shifted = (image - center * newest) / half_width
            later = 2.0 * shifted - history[:, columns].astype(jnp.float32)
            fresh = jnp.where(first, shifted, later).astype(jnp.bfloat16)
            history[:, columns] = old
            extended[:, columns] = fresh
        return carry

    history[...] = jnp.zeros_like(history)
    lax.fori_loop(0, DEGREE, one_step, 0)
    out_ref[...] = extended[:, :nodes]


def filtered_states(orbitals, cell_matrix, connectivity, surface_nodes, cell_scale, potential):
    states, nodes = orbitals.shape
    cells, node_cell = connectivity.shape
    surf = surface_nodes.shape[1]
    vmem = pl.BlockSpec(memory_space=pltpu.VMEM)
    smem = pl.BlockSpec(memory_space=pltpu.SMEM)
    bf16, f32 = jnp.bfloat16, jnp.float32
    return pl.pallas_call(
        functools.partial(filter_kernel, lax.axis_size("dom"), cells - cells // 4),
        out_shape=jax.ShapeDtypeStruct((states, nodes), bf16),
        in_specs=[vmem, vmem, vmem, vmem, smem, vmem],
        out_specs=vmem,
        scratch_shapes=[
            pltpu.VMEM((states, nodes + surf), bf16),
            pltpu.VMEM((states, nodes), bf16),
            pltpu.VMEM((states, nodes + surf), f32),
            pltpu.VMEM((nodes + surf, cells * node_cell), bf16),
            pltpu.VMEM((nodes, surf), bf16),
            pltpu.VMEM((2 * states, cells * node_cell), bf16),
            pltpu.VMEM((DEGREE, states, surf), bf16),
            pltpu.VMEM((DEGREE, states, surf), bf16),
            pltpu.VMEM((DEGREE, states, surf), f32),
            pltpu.VMEM((DEGREE, states, surf), f32),
        ] + [pltpu.SemaphoreType.DMA((DEGREE,))] * 4,
        compiler_params=pltpu.CompilerParams(
            collective_id=0, has_side_effects=True, vmem_limit_bytes=52 * 1024 * 1024
        ),
        name="chebyshev_filter",
    )(orbitals, cell_matrix, connectivity, surface_nodes, cell_scale, potential[None, :])


def product(left, right):
    left_high = left.astype(jnp.bfloat16)
    left_low = (left - left_high.astype(jnp.float32)).astype(jnp.bfloat16)
    right_high = right.astype(jnp.bfloat16)
    right_low = (right - right_high.astype(jnp.float32)).astype(jnp.bfloat16)
    dot = functools.partial(jnp.dot, preferred_element_type=jnp.float32)
    return dot(left_high, right_high) + (dot(left_high, right_low) + dot(left_low, right_high))


def tail_kernel(
    n_dom, n_st, node_total,
    f_ref, out_ref,
    slabs, gram_out, gram_in, chunk_out, chunk_in, gathered, gram_ref, growing_ref, inverse_ref,
    rotation_ref, rotated, *sems,
):
    (slab_send, slab_recv, gram_send, gram_recv, chunk_send, chunk_recv,
     dom_send, dom_recv, st_send, st_recv, out_send, out_recv) = sems
    states, nodes = f_ref.shape
    part = nodes // n_st
    rows = states // n_dom
    states_all = states * n_st
    d, q = lax.axis_index("dom"), lax.axis_index("st")

    def peer(k):
        return lax.rem(q + k, n_st)

    def along(j):
        return lax.rem(d + j, n_dom)

    barrier = pltpu.get_barrier_semaphore()
    for k in range(1, n_st):
        pl.semaphore_signal(barrier, inc=1, device_id={"st": peer(k)}, device_id_type=MESH)
    for j in range(1, n_dom):
        pl.semaphore_signal(barrier, inc=1, device_id={"dom": along(j)}, device_id_type=MESH)
    pl.semaphore_wait(barrier, n_st + n_dom - 2)

    def send(src, dst, send_sem, recv_sem, target):
        copy = pltpu.make_async_remote_copy(
            src_ref=src, dst_ref=dst, send_sem=send_sem, recv_sem=recv_sem,
            device_id=target, device_id_type=MESH,
        )
        copy.start()
        return copy

    def columns(p):
        return pl.ds(pl.multiple_of(p * part, part), part)

    def band(p):
        return pl.ds(pl.multiple_of(p * states, states), states)

    sent = []
    slab = [
        send(f_ref.at[:, columns(peer(k))], slabs.at[band(q), :],
             slab_send.at[k], slab_recv.at[k], {"st": peer(k)})
        for k in range(1, n_st)
    ]
    slabs[band(q), :] = f_ref[:, columns(q)]
    for copy in slab:
        copy.wait()

    def gram_rows(p):
        return lax.dot_general(slabs[band(p), :], slabs[...], NT, preferred_element_type=jnp.float32)

    grams = []
    for k in range(1, n_st):
        gram_out[k] = gram_rows(peer(k))
        grams.append(send(gram_out.at[k], gram_in.at[k], gram_send.at[k], gram_recv.at[k],
                          {"st": peer(k)}))
    total = gram_rows(q)
    for k in range(1, n_st):
        grams[k - 1].wait()
        total += gram_in[k]
    for j in range(n_dom):
        chunk_out[j] = total[j * rows:(j + 1) * rows]
    chunks = [
        send(chunk_out.at[along(j)], chunk_in.at[j], chunk_send.at[j], chunk_recv.at[j],
             {"dom": along(j)})
        for j in range(1, n_dom)
    ]
    mine = chunk_out[d]
    for j in range(1, n_dom):
        chunks[j - 1].wait()
        mine += chunk_in[j]
    gathered[q, d] = mine

    def spread(source, slot):
        return [
            send(gathered.at[q, source], gathered.at[q, source],
                 st_send.at[k, slot], st_recv.at[k, slot], {"st": peer(k)})
            for k in range(1, n_st)
        ]

    doms = [
        send(gathered.at[q, d], gathered.at[q, d], dom_send.at[j], dom_recv.at[j],
             {"dom": along(j)})
        for j in range(1, n_dom)
    ]
    sent = spread(d, 0)
    for j in range(1, n_dom):
        doms[j - 1].wait_recv()
        sent += spread(lax.rem(d + n_dom - j, n_dom), j)
    for copy in doms:
        copy.wait_send()
    for copy in sent:
        copy.wait()
    for p in range(n_st):
        for j in range(n_dom):
            start = p * states + j * rows
            gram_ref[start:start + rows, :] = gathered[p, j]

    gram = gram_ref[...]
    scale_sum = jnp.sqrt(jnp.sum(gram * gram, keepdims=True)) + epsilon
    shape = (states_all, states_all)
    identity = jnp.where(
        lax.broadcasted_iota(jnp.int32, shape, 0) == lax.broadcasted_iota(jnp.int32, shape, 1),
        1.0, 0.0,
    )
    growing_ref[...] = gram / scale_sum
    for iteration in range(ROOT_ITERS):
        if iteration == 0:
            factor = 1.5 * identity - 0.5 * growing_ref[...]
            inverse = factor
        else:
            factor = 1.5 * identity - 0.5 * product(inverse_ref[...], growing_ref[...])
            inverse = product(factor, inverse_ref[...])
        if iteration < ROOT_ITERS - 1:
            growing_ref[...] = product(growing_ref[...], factor)
        inverse_ref[...] = inverse
    rotation_ref[...] = jnp.transpose(
        inverse_ref[...] * jnp.sqrt(node_total / scale_sum)
    ).astype(jnp.bfloat16)

    def rotate(p):
        return jnp.dot(
            rotation_ref[band(p), :], slabs[...], preferred_element_type=jnp.float32
        ).astype(jnp.bfloat16)

    outs = []
    for k in range(1, n_st):
        rotated[k] = rotate(peer(k))
        outs.append(send(rotated.at[k], out_ref.at[:, columns(q)], out_send.at[k], out_recv.at[k],
                         {"st": peer(k)}))
    out_ref[:, columns(q)] = rotate(q)
    for copy in outs:
        copy.wait()


def tail_in_kernel(newest):
    n_dom, n_st = lax.axis_size("dom"), lax.axis_size("st")
    states, nodes = newest.shape
    part, rows, states_all = nodes // n_st, states // n_dom, states * n_st
    vmem = pl.BlockSpec(memory_space=pltpu.VMEM)
    bf16, f32 = jnp.bfloat16, jnp.float32
    square = pltpu.VMEM((states_all, states_all), f32)
    return pl.pallas_call(
        functools.partial(tail_kernel, n_dom, n_st, float(n_dom * nodes)),
        out_shape=jax.ShapeDtypeStruct((states, nodes), bf16),
        in_specs=[vmem],
        out_specs=vmem,
        scratch_shapes=[
            pltpu.VMEM((states_all, part), bf16),
            pltpu.VMEM((n_st, states, states_all), f32),
            pltpu.VMEM((n_st, states, states_all), f32),
            pltpu.VMEM((n_dom, rows, states_all), f32),
            pltpu.VMEM((n_dom, rows, states_all), f32),
            pltpu.VMEM((n_st, n_dom, rows, states_all), f32),
            square, square, square,
            pltpu.VMEM((states_all, states_all), bf16),
            pltpu.VMEM((n_st, states, part), bf16),
        ] + [pltpu.SemaphoreType.DMA((n_st,))] * 4
        + [pltpu.SemaphoreType.DMA((n_dom,))] * 4
        + [pltpu.SemaphoreType.DMA((n_st, n_dom))] * 2
        + [pltpu.SemaphoreType.DMA((n_st,))] * 2,
        compiler_params=pltpu.CompilerParams(
            collective_id=1, has_side_effects=True, vmem_limit_bytes=40 * 1024 * 1024
        ),
        name="gram_and_rotation",
    )(newest)


def newton_root(gram):
    highest = lax.Precision.HIGHEST
    states_all = gram.shape[0]
    scale_sum = jnp.sqrt(jnp.sum(gram * gram)) + epsilon
    identity = jnp.eye(states_all, dtype=jnp.float32)
    growing = gram / scale_sum
    inverse = identity
    for iteration in range(ROOT_ITERS):
        factor = 1.5 * identity - 0.5 * jnp.dot(inverse, growing, precision=highest)
        growing = jnp.dot(growing, factor, precision=highest)
        inverse = jnp.dot(factor, inverse, precision=highest)
    return (inverse, scale_sum)


def tail_in_parts(newest):
    slabs = lax.all_to_all(newest, "st", split_axis=1, concat_axis=0, tiled=True)
    gram_part = jnp.dot(slabs, slabs.T, preferred_element_type=jnp.float32)
    row_block = lax.psum_scatter(gram_part, "st", scatter_dimension=0, tiled=True)
    row_block = lax.psum(row_block, "dom")
    gram = lax.all_gather(row_block, "st", axis=0, tiled=True)
    inverse, scale_sum = newton_root(gram)
    node_total = lax.axis_size("dom") * newest.shape[1]
    rotation = (inverse * jnp.sqrt(node_total / scale_sum)).astype(jnp.bfloat16)
    rotated = jnp.dot(rotation.T, slabs, preferred_element_type=jnp.float32).astype(jnp.bfloat16)
    return lax.all_to_all(rotated, "st", split_axis=0, concat_axis=1, tiled=True)


def body(orbitals, cell_matrix, connectivity, surface_nodes, cell_scale, potential):
    newest = filtered_states(
        orbitals, cell_matrix, connectivity, surface_nodes, cell_scale, potential
    )
    if orbitals.shape[0] % lax.axis_size("dom") == 0:
        return tail_in_kernel(newest)
    return tail_in_parts(newest)


def solution(mesh):
    return jax.shard_map(
        body,
        mesh=mesh,
        in_specs=(P("st", "dom"), P(), P("dom", None), P("dom", None), P("dom"), P("dom")),
        out_specs=P("st", "dom"),
        check_vma=False,
    )
```

```python
import functools

import jax
import jax.numpy as jnp
from jax import lax
from jax.experimental import pallas as pl
from jax.experimental.pallas import tpu as pltpu
from jax.sharding import PartitionSpec as P

DEGREE = 3
ROOT_ITERS = 4
MESH = pl.DeviceIdType.MESH

center = 7.0
half_width = 6.0
epsilon = 1e-06

NT = (((1,), (1,)), ((), ()))


def halves(values):
    high = values.astype(jnp.bfloat16)
    low = (values - high.astype(jnp.float32)).astype(jnp.bfloat16)
    return jnp.concatenate([high, low], axis=0)


def filter_kernel(
    n_dom, inner,
    f_hbm, matrix_hbm, conn_hbm, surface_hbm, scale_ref, potential_hbm, out_ref,
    matrix_ref, conn_ref, surface_ref, potential_ref, extended, history, totals, picks, surface_pick, pair, edge_out, edge_in, back_out, back_in,
    edge_send, edge_recv, back_send, back_recv, load_sems,
):
    states, nodes = f_hbm.shape
    surf = surface_ref.shape[1]
    cells, node_cell = conn_ref.shape
    width = nodes + surf
    tile = 256
    me = lax.axis_index("dom")
    after, before = lax.rem(me + 1, n_dom), lax.rem(me + n_dom - 1, n_dom)

    barrier = pltpu.get_barrier_semaphore()
    for neighbour in (after, before):
        pl.semaphore_signal(barrier, inc=1, device_id={"dom": neighbour}, device_id_type=MESH)

    loads = [
        pltpu.make_async_copy(src, dst, load_sems.at[index])
        for index, (src, dst) in enumerate([
            (conn_hbm, conn_ref), (surface_hbm, surface_ref),
            (f_hbm, extended.at[:, pl.ds(0, nodes)]), (matrix_hbm, matrix_ref),
            (potential_hbm, potential_ref),
        ])
    ]
    for load in loads:
        load.start()

    def one_hot(ids, start):
        columns = ids.shape[1]
        node = lax.broadcasted_iota(jnp.int32, (tile, columns), 0).astype(jnp.bfloat16)
        wanted = jnp.broadcast_to((ids - start).astype(jnp.bfloat16), (tile, columns))
        one, zero = jnp.bfloat16(1), jnp.bfloat16(0)
        return jnp.where(node == wanted, one, zero)

    loads[0].wait()
    ids_down = jnp.transpose(conn_ref[...].astype(jnp.float32))
    for cell in range(cells):
        wanted = jnp.broadcast_to(ids_down[:, cell:cell + 1], (node_cell, tile))
        lanes = lax.broadcasted_iota(jnp.int32, (node_cell, tile), 1).astype(jnp.bfloat16)
        rows = pl.ds(cell * node_cell, node_cell)

        def build_tile(index, carry):
            start = index * tile
            shifted = (wanted - start.astype(jnp.float32)).astype(jnp.bfloat16)
            picks[rows, pl.ds(pl.multiple_of(start, tile), tile)] = jnp.where(
                lanes == shifted, jnp.bfloat16(1), jnp.bfloat16(0)
            )
            return carry

        lax.fori_loop(0, (nodes if cell < inner else width) // tile, build_tile, 0)
    for load in loads[1:]:
        load.wait()
    for start in range(0, nodes, tile):
        surface_pick[pl.ds(start, tile), :] = one_hot(surface_ref[...], start)

    def run_cells(first, last, extent):
        count = last - first
        gathered = []
        for cell in range(first, last):
            ids = conn_ref[pl.ds(cell, 1), :]
            found = jnp.zeros((states, node_cell), jnp.float32)
            for start in range(0, extent, tile):
                found += jnp.dot(
                    extended[:, start:start + tile], one_hot(ids, start),
                    preferred_element_type=jnp.float32,
                )
            gathered.append(found.astype(jnp.bfloat16))
        products = jnp.dot(
            jnp.concatenate(gathered, axis=0), matrix_ref[...], preferred_element_type=jnp.float32
        )
        for index in range(count):
            scaled = products[index * states:(index + 1) * states] * scale_ref[first + index]
            pair[:, index * node_cell:(index + 1) * node_cell] = halves(scaled)
        group = pl.ds(first * node_cell, count * node_cell)

        def scatter_tile(index, carry):
            columns = pl.ds(pl.multiple_of(index * tile, tile), tile)
            spread = jnp.dot(
                pair[:, :count * node_cell], picks[group, columns],
                preferred_element_type=jnp.float32,
            )
            totals[:, columns] += spread[:states] + spread[states:]
            return carry

        lax.fori_loop(0, extent // tile, scatter_tile, 0)

    pl.semaphore_wait(barrier, 2)

    def one_step(step, carry):
        edge_out[step] = jnp.dot(
            extended[:, :nodes], surface_pick[...], preferred_element_type=jnp.float32
        ).astype(jnp.bfloat16)
        edge = pltpu.make_async_remote_copy(
            src_ref=edge_out.at[step], dst_ref=edge_in.at[step],
            send_sem=edge_send.at[step], recv_sem=edge_recv.at[step],
            device_id={"dom": before}, device_id_type=MESH,
        )
        edge.start()
        totals[...] = jnp.zeros_like(totals)
        run_cells(0, inner // 2, nodes)
        edge.wait()
        ghosts = edge_in[step]
        extended[:, nodes:] = jnp.where(me == n_dom - 1, jnp.zeros_like(ghosts), ghosts)
        run_cells(inner, cells, width)
        back_out[step] = totals[:, nodes:]
        back = pltpu.make_async_remote_copy(
            src_ref=back_out.at[step], dst_ref=back_in.at[step],
            send_sem=back_send.at[step], recv_sem=back_recv.at[step],
            device_id={"dom": after}, device_id_type=MESH,
        )
        back.start()
        run_cells(inner // 2, inner, nodes)
        back.wait()
        returned = back_in[step]
        returned = jnp.where(me == 0, jnp.zeros_like(returned), returned)
        parts = halves(returned)
        first = step == 0
        for start in range(0, nodes, tile):
            columns = pl.ds(start, tile)
            spread = lax.dot_general(
                parts, surface_pick[columns, :], NT, preferred_element_type=jnp.float32
            )
            total = totals[:, columns] + (spread[:states] + spread[states:])
            old = extended[:, columns]
            newest = old.astype(jnp.float32)
            image = total + potential_ref[:, columns] * newest
            shifted = (image - center * newest) / half_width
            later = 2.0 * shifted - history[:, columns].astype(jnp.float32)
            fresh = jnp.where(first, shifted, later).astype(jnp.bfloat16)
            history[:, columns] = old
            extended[:, columns] = fresh
        return carry

    history[...] = jnp.zeros_like(history)
    lax.fori_loop(0, DEGREE, one_step, 0)
    out_ref[...] = extended[:, :nodes]


def filtered_states(orbitals, cell_matrix, connectivity, surface_nodes, cell_scale, potential):
    states, nodes = orbitals.shape
    cells, node_cell = connectivity.shape
    surf = surface_nodes.shape[1]
    vmem = pl.BlockSpec(memory_space=pltpu.VMEM)
    smem = pl.BlockSpec(memory_space=pltpu.SMEM)
    hbm = pl.BlockSpec(memory_space=pl.ANY)
    bf16, f32 = jnp.bfloat16, jnp.float32
    return pl.pallas_call(
        functools.partial(filter_kernel, lax.axis_size("dom"), cells - cells // 4),
        out_shape=jax.ShapeDtypeStruct((states, nodes), bf16),
        in_specs=[hbm, hbm, hbm, hbm, smem, hbm],
        out_specs=vmem,
        scratch_shapes=[
            pltpu.VMEM((node_cell, node_cell), bf16),
            pltpu.VMEM((cells, node_cell), jnp.int32),
            pltpu.VMEM((1, surf), jnp.int32),
            pltpu.VMEM((1, nodes), f32),
            pltpu.VMEM((states, nodes + surf), bf16),
            pltpu.VMEM((states, nodes), bf16),
            pltpu.VMEM((states, nodes + surf), f32),
            pltpu.VMEM((cells * node_cell, nodes + surf), bf16),
            pltpu.VMEM((nodes, surf), bf16),
            pltpu.VMEM((2 * states, cells * node_cell), bf16),
            pltpu.VMEM((DEGREE, states, surf), bf16),
            pltpu.VMEM((DEGREE, states, surf), bf16),
            pltpu.VMEM((DEGREE, states, surf), f32),
            pltpu.VMEM((DEGREE, states, surf), f32),
        ] + [pltpu.SemaphoreType.DMA((DEGREE,))] * 4 + [pltpu.SemaphoreType.DMA((5,))],
        compiler_params=pltpu.CompilerParams(
            collective_id=0, has_side_effects=True, vmem_limit_bytes=52 * 1024 * 1024
        ),
        name="chebyshev_filter",
    )(orbitals, cell_matrix, connectivity, surface_nodes, cell_scale, potential[None, :])


def product(left, right):
    left_high = left.astype(jnp.bfloat16)
    left_low = (left - left_high.astype(jnp.float32)).astype(jnp.bfloat16)
    right_high = right.astype(jnp.bfloat16)
    right_low = (right - right_high.astype(jnp.float32)).astype(jnp.bfloat16)
    dot = functools.partial(jnp.dot, preferred_element_type=jnp.float32)
    return dot(left_high, right_high) + (dot(left_high, right_low) + dot(left_low, right_high))


def tail_kernel(
    n_dom, n_st, node_total,
    f_ref, out_ref,
    slabs, gram_out, gram_in, chunk_out, chunk_in, gathered, gram_ref, growing_ref, inverse_ref,
    rotation_ref, rotated, *sems,
):
    (slab_send, slab_recv, gram_send, gram_recv, chunk_send, chunk_recv,
     dom_send, dom_recv, st_send, st_recv, out_send, out_recv) = sems
    states, nodes = f_ref.shape
    part = nodes // n_st
    rows = states // n_dom
    states_all = states * n_st
    d, q = lax.axis_index("dom"), lax.axis_index("st")

    def peer(k):
        return lax.rem(q + k, n_st)

    def along(j):
        return lax.rem(d + j, n_dom)

    barrier = pltpu.get_barrier_semaphore()
    for k in range(1, n_st):
        pl.semaphore_signal(barrier, inc=1, device_id={"st": peer(k)}, device_id_type=MESH)
    for j in range(1, n_dom):
        pl.semaphore_signal(barrier, inc=1, device_id={"dom": along(j)}, device_id_type=MESH)
    pl.semaphore_wait(barrier, n_st + n_dom - 2)

    def send(src, dst, send_sem, recv_sem, target):
        copy = pltpu.make_async_remote_copy(
            src_ref=src, dst_ref=dst, send_sem=send_sem, recv_sem=recv_sem,
            device_id=target, device_id_type=MESH,
        )
        copy.start()
        return copy

    def columns(p):
        return pl.ds(pl.multiple_of(p * part, part), part)

    def band(p):
        return pl.ds(pl.multiple_of(p * states, states), states)

    sent = []
    slab = [
        send(f_ref.at[:, columns(peer(k))], slabs.at[band(q), :],
             slab_send.at[k], slab_recv.at[k], {"st": peer(k)})
        for k in range(1, n_st)
    ]
    slabs[band(q), :] = f_ref[:, columns(q)]
    for copy in slab:
        copy.wait()

    def gram_rows(p):
        return lax.dot_general(slabs[band(p), :], slabs[...], NT, preferred_element_type=jnp.float32)

    grams = []
    for k in range(1, n_st):
        gram_out[k] = gram_rows(peer(k))
        grams.append(send(gram_out.at[k], gram_in.at[k], gram_send.at[k], gram_recv.at[k],
                          {"st": peer(k)}))
    total = gram_rows(q)
    for k in range(1, n_st):
        grams[k - 1].wait()
        total += gram_in[k]
    for j in range(n_dom):
        chunk_out[j] = total[j * rows:(j + 1) * rows]
    chunks = [
        send(chunk_out.at[along(j)], chunk_in.at[j], chunk_send.at[j], chunk_recv.at[j],
             {"dom": along(j)})
        for j in range(1, n_dom)
    ]
    mine = chunk_out[d]
    for j in range(1, n_dom):
        chunks[j - 1].wait()
        mine += chunk_in[j]
    gathered[q, d] = mine

    def spread(source, slot):
        return [
            send(gathered.at[q, source], gathered.at[q, source],
                 st_send.at[k, slot], st_recv.at[k, slot], {"st": peer(k)})
            for k in range(1, n_st)
        ]

    doms = [
        send(gathered.at[q, d], gathered.at[q, d], dom_send.at[j], dom_recv.at[j],
             {"dom": along(j)})
        for j in range(1, n_dom)
    ]
    sent = spread(d, 0)
    for j in range(1, n_dom):
        doms[j - 1].wait_recv()
        sent += spread(lax.rem(d + n_dom - j, n_dom), j)
    for copy in doms:
        copy.wait_send()
    for copy in sent:
        copy.wait()
    for p in range(n_st):
        for j in range(n_dom):
            start = p * states + j * rows
            gram_ref[start:start + rows, :] = gathered[p, j]

    gram = gram_ref[...]
    scale_sum = jnp.sqrt(jnp.sum(gram * gram, keepdims=True)) + epsilon
    shape = (states_all, states_all)
    identity = jnp.where(
        lax.broadcasted_iota(jnp.int32, shape, 0) == lax.broadcasted_iota(jnp.int32, shape, 1),
        1.0, 0.0,
    )
    growing_ref[...] = gram / scale_sum
    for iteration in range(ROOT_ITERS):
        if iteration == 0:
            factor = 1.5 * identity - 0.5 * growing_ref[...]
            inverse = factor
        else:
            factor = 1.5 * identity - 0.5 * product(inverse_ref[...], growing_ref[...])
            inverse = product(factor, inverse_ref[...])
        if iteration < ROOT_ITERS - 1:
            growing_ref[...] = product(growing_ref[...], factor)
        inverse_ref[...] = inverse
    rotation_ref[...] = jnp.transpose(
        inverse_ref[...] * jnp.sqrt(node_total / scale_sum)
    ).astype(jnp.bfloat16)

    def rotate(p):
        return jnp.dot(
            rotation_ref[band(p), :], slabs[...], preferred_element_type=jnp.float32
        ).astype(jnp.bfloat16)

    outs = []
    for k in range(1, n_st):
        rotated[k] = rotate(peer(k))
        outs.append(send(rotated.at[k], out_ref.at[:, columns(q)], out_send.at[k], out_recv.at[k],
                         {"st": peer(k)}))
    out_ref[:, columns(q)] = rotate(q)
    for copy in outs:
        copy.wait()


def tail_in_kernel(newest):
    n_dom, n_st = lax.axis_size("dom"), lax.axis_size("st")
    states, nodes = newest.shape
    part, rows, states_all = nodes // n_st, states // n_dom, states * n_st
    vmem = pl.BlockSpec(memory_space=pltpu.VMEM)
    bf16, f32 = jnp.bfloat16, jnp.float32
    square = pltpu.VMEM((states_all, states_all), f32)
    return pl.pallas_call(
        functools.partial(tail_kernel, n_dom, n_st, float(n_dom * nodes)),
        out_shape=jax.ShapeDtypeStruct((states, nodes), bf16),
        in_specs=[vmem],
        out_specs=vmem,
        scratch_shapes=[
            pltpu.VMEM((states_all, part), bf16),
            pltpu.VMEM((n_st, states, states_all), f32),
            pltpu.VMEM((n_st, states, states_all), f32),
            pltpu.VMEM((n_dom, rows, states_all), f32),
            pltpu.VMEM((n_dom, rows, states_all), f32),
            pltpu.VMEM((n_st, n_dom, rows, states_all), f32),
            square, square, square,
            pltpu.VMEM((states_all, states_all), bf16),
            pltpu.VMEM((n_st, states, part), bf16),
        ] + [pltpu.SemaphoreType.DMA((n_st,))] * 4
        + [pltpu.SemaphoreType.DMA((n_dom,))] * 4
        + [pltpu.SemaphoreType.DMA((n_st, n_dom))] * 2
        + [pltpu.SemaphoreType.DMA((n_st,))] * 2,
        compiler_params=pltpu.CompilerParams(
            collective_id=1, has_side_effects=True, vmem_limit_bytes=40 * 1024 * 1024
        ),
        name="gram_and_rotation",
    )(newest)


def newton_root(gram):
    highest = lax.Precision.HIGHEST
    states_all = gram.shape[0]
    scale_sum = jnp.sqrt(jnp.sum(gram * gram)) + epsilon
    identity = jnp.eye(states_all, dtype=jnp.float32)
    growing = gram / scale_sum
    inverse = identity
    for iteration in range(ROOT_ITERS):
        factor = 1.5 * identity - 0.5 * jnp.dot(inverse, growing, precision=highest)
        growing = jnp.dot(growing, factor, precision=highest)
        inverse = jnp.dot(factor, inverse, precision=highest)
    return (inverse, scale_sum)


def tail_in_parts(newest):
    slabs = lax.all_to_all(newest, "st", split_axis=1, concat_axis=0, tiled=True)
    gram_part = jnp.dot(slabs, slabs.T, preferred_element_type=jnp.float32)
    row_block = lax.psum_scatter(gram_part, "st", scatter_dimension=0, tiled=True)
    row_block = lax.psum(row_block, "dom")
    gram = lax.all_gather(row_block, "st", axis=0, tiled=True)
    inverse, scale_sum = newton_root(gram)
    node_total = lax.axis_size("dom") * newest.shape[1]
    rotation = (inverse * jnp.sqrt(node_total / scale_sum)).astype(jnp.bfloat16)
    rotated = jnp.dot(rotation.T, slabs, preferred_element_type=jnp.float32).astype(jnp.bfloat16)
    return lax.all_to_all(rotated, "st", split_axis=0, concat_axis=1, tiled=True)


def body(orbitals, cell_matrix, connectivity, surface_nodes, cell_scale, potential):
    newest = filtered_states(
        orbitals, cell_matrix, connectivity, surface_nodes, cell_scale, potential
    )
    if orbitals.shape[0] % lax.axis_size("dom") == 0:
        return tail_in_kernel(newest)
    return tail_in_parts(newest)


def solution(mesh):
    return jax.shard_map(
        body,
        mesh=mesh,
        in_specs=(P("st", "dom"), P(), P("dom", None), P("dom", None), P("dom"), P("dom")),
        out_specs=P("st", "dom"),
        check_vma=False,
    )
```

```python
import functools

import jax
import jax.numpy as jnp
from jax import lax
from jax.experimental import pallas as pl
from jax.experimental.pallas import tpu as pltpu
from jax.sharding import PartitionSpec as P

DEGREE = 3
ROOT_ITERS = 4
MESH = pl.DeviceIdType.MESH

center = 7.0
half_width = 6.0
epsilon = 1e-06

NT = (((1,), (1,)), ((), ()))


def halves(values):
    high = values.astype(jnp.bfloat16)
    low = (values - high.astype(jnp.float32)).astype(jnp.bfloat16)
    return jnp.concatenate([high, low], axis=0)


def greet(n_dom, n_st, everyone):
    d, q = lax.axis_index("dom"), lax.axis_index("st")
    barrier = pltpu.get_barrier_semaphore()
    steps = range(1, n_dom) if everyone else (1, n_dom - 1)
    for j in steps:
        pl.semaphore_signal(
            barrier, inc=1, device_id={"dom": lax.rem(d + j, n_dom)}, device_id_type=MESH
        )
    if everyone:
        for k in range(1, n_st):
            pl.semaphore_signal(
                barrier, inc=1, device_id={"st": lax.rem(q + k, n_st)}, device_id_type=MESH
            )
    return barrier, len(steps) + (n_st - 1 if everyone else 0)


def kernel(
    n_dom, n_st, inner, with_tail,
    f_hbm, matrix_hbm, conn_hbm, surface_hbm, scale_ref, potential_hbm, out_ref,
    matrix_ref, conn_ref, surface_ref, potential_ref, extended, history, totals, picks, surface_pick, pair, edge_out, edge_in, back_out, back_in,
    edge_send, edge_recv, back_send, back_recv, load_sems, *tail_refs,
):
    states, nodes = f_hbm.shape
    surf = surface_ref.shape[1]
    cells, node_cell = conn_ref.shape
    width = nodes + surf
    tile = 256
    me = lax.axis_index("dom")
    after, before = lax.rem(me + 1, n_dom), lax.rem(me + n_dom - 1, n_dom)

    barrier, greetings = greet(n_dom, n_st, with_tail)
    loads = [
        pltpu.make_async_copy(src, dst, load_sems.at[index])
        for index, (src, dst) in enumerate([
            (conn_hbm, conn_ref), (surface_hbm, surface_ref),
            (f_hbm, extended.at[:, pl.ds(0, nodes)]), (matrix_hbm, matrix_ref),
            (potential_hbm, potential_ref),
        ])
    ]
    for load in loads:
        load.start()

    def one_hot(ids, start):
        columns = ids.shape[1]
        node = lax.broadcasted_iota(jnp.int32, (tile, columns), 0).astype(jnp.bfloat16)
        wanted = jnp.broadcast_to((ids - start).astype(jnp.bfloat16), (tile, columns))
        one, zero = jnp.bfloat16(1), jnp.bfloat16(0)
        return jnp.where(node == wanted, one, zero)

    loads[0].wait()
    ids_down = jnp.transpose(conn_ref[...].astype(jnp.float32))
    for cell in range(cells):
        wanted = jnp.broadcast_to(ids_down[:, cell:cell + 1], (node_cell, tile))
        lanes = lax.broadcasted_iota(jnp.int32, (node_cell, tile), 1).astype(jnp.bfloat16)
        rows = pl.ds(cell * node_cell, node_cell)

        def build_tile(index, carry):
            start = index * tile
            shifted = (wanted - start.astype(jnp.float32)).astype(jnp.bfloat16)
            picks[rows, pl.ds(pl.multiple_of(start, tile), tile)] = jnp.where(
                lanes == shifted, jnp.bfloat16(1), jnp.bfloat16(0)
            )
            return carry

        lax.fori_loop(0, (nodes if cell < inner else width) // tile, build_tile, 0)
    for load in loads[1:]:
        load.wait()
    for start in range(0, nodes, tile):
        surface_pick[pl.ds(start, tile), :] = one_hot(surface_ref[...], start)

    def run_cells(first, last, extent):
        count = last - first
        gathered = []
        for cell in range(first, last):
            ids = conn_ref[pl.ds(cell, 1), :]
            found = jnp.zeros((states, node_cell), jnp.float32)
            for start in range(0, extent, tile):
                found += jnp.dot(
                    extended[:, start:start + tile], one_hot(ids, start),
                    preferred_element_type=jnp.float32,
                )
            gathered.append(found.astype(jnp.bfloat16))
        products = jnp.dot(
            jnp.concatenate(gathered, axis=0), matrix_ref[...], preferred_element_type=jnp.float32
        )
        for index in range(count):
            scaled = products[index * states:(index + 1) * states] * scale_ref[first + index]
            pair[:, index * node_cell:(index + 1) * node_cell] = halves(scaled)
        group = pl.ds(first * node_cell, count * node_cell)

        for start in range(0, extent, tile):
            columns = pl.ds(start, tile)
            spread = jnp.dot(
                pair[:, :count * node_cell], picks[group, columns],
                preferred_element_type=jnp.float32,
            )
            totals[:, columns] += spread[:states] + spread[states:]

    pl.semaphore_wait(barrier, greetings)

    def one_step(step, carry):
        edge_out[step] = jnp.dot(
            extended[:, :nodes], surface_pick[...], preferred_element_type=jnp.float32
        ).astype(jnp.bfloat16)
        edge = pltpu.make_async_remote_copy(
            src_ref=edge_out.at[step], dst_ref=edge_in.at[step],
            send_sem=edge_send.at[step], recv_sem=edge_recv.at[step],
            device_id={"dom": before}, device_id_type=MESH,
        )
        edge.start()
        totals[...] = jnp.zeros_like(totals)
        run_cells(0, inner // 2, nodes)
        edge.wait()
        ghosts = edge_in[step]
        extended[:, nodes:] = jnp.where(me == n_dom - 1, jnp.zeros_like(ghosts), ghosts)
        run_cells(inner, cells, width)
        back_out[step] = totals[:, nodes:]
        back = pltpu.make_async_remote_copy(
            src_ref=back_out.at[step], dst_ref=back_in.at[step],
            send_sem=back_send.at[step], recv_sem=back_recv.at[step],
            device_id={"dom": after}, device_id_type=MESH,
        )
        back.start()
        run_cells(inner // 2, inner, nodes)
        back.wait()
        returned = back_in[step]
        returned = jnp.where(me == 0, jnp.zeros_like(returned), returned)
        parts = halves(returned)
        first = step == 0
        for start in range(0, nodes, tile):
            columns = pl.ds(start, tile)
            spread = lax.dot_general(
                parts, surface_pick[columns, :], NT, preferred_element_type=jnp.float32
            )
            total = totals[:, columns] + (spread[:states] + spread[states:])
            old = extended[:, columns]
            newest = old.astype(jnp.float32)
            image = total + potential_ref[:, columns] * newest
            shifted = (image - center * newest) / half_width
            later = 2.0 * shifted - history[:, columns].astype(jnp.float32)
            fresh = jnp.where(first, shifted, later).astype(jnp.bfloat16)
            history[:, columns] = old
            extended[:, columns] = fresh
        return carry

    history[...] = jnp.zeros_like(history)
    lax.fori_loop(0, DEGREE, one_step, 0)
    if with_tail:
        tail_part(n_dom, n_st, float(n_dom * nodes), states, nodes, extended, out_ref, *tail_refs)
    else:
        out_ref[...] = extended[:, :nodes]


def product(left, right):
    left_high = left.astype(jnp.bfloat16)
    left_low = (left - left_high.astype(jnp.float32)).astype(jnp.bfloat16)
    right_high = right.astype(jnp.bfloat16)
    right_low = (right - right_high.astype(jnp.float32)).astype(jnp.bfloat16)
    dot = functools.partial(jnp.dot, preferred_element_type=jnp.float32)
    return dot(left_high, right_high) + (dot(left_high, right_low) + dot(left_low, right_high))


def tail_part(
    n_dom, n_st, node_total, states, nodes,
    f_ref, out_ref,
    full, gram_out, gram_in, chunk_out, chunk_in, gathered, gram_ref, growing_ref, inverse_ref,
    *sems,
):
    (slab_send, slab_recv, gram_send, gram_recv, chunk_send, chunk_recv,
     dom_send, dom_recv, st_send, st_recv, rest_send, rest_recv) = sems
    part = nodes // n_st
    rows = states // n_dom
    states_all = states * n_st
    d, q = lax.axis_index("dom"), lax.axis_index("st")

    def peer(k):
        return lax.rem(q + k, n_st)

    def along(j):
        return lax.rem(d + j, n_dom)

    def send(src, dst, send_sem, recv_sem, target):
        copy = pltpu.make_async_remote_copy(
            src_ref=src, dst_ref=dst, send_sem=send_sem, recv_sem=recv_sem,
            device_id=target, device_id_type=MESH,
        )
        copy.start()
        return copy

    def columns(p):
        return pl.ds(pl.multiple_of(p * part, part), part)

    def band(p):
        return pl.ds(pl.multiple_of(p * states, states), states)

    slab = [
        send(f_ref.at[:, columns(peer(k))], full.at[band(q), columns(peer(k))],
             slab_send.at[k], slab_recv.at[k], {"st": peer(k)})
        for k in range(1, n_st)
    ]

    def send_rest(m):
        return [
            send(f_ref.at[:, columns(peer(k + m))], full.at[band(q), columns(peer(k + m))],
                 rest_send.at[k, m], rest_recv.at[k, m], {"st": peer(k)})
            for k in range(1, n_st)
        ]

    full[band(q), :] = f_ref[:, :nodes]
    for copy in slab:
        copy.wait()

    def gram_rows(p):
        return lax.dot_general(
            full[band(p), columns(q)], full[:, columns(q)], NT,
            preferred_element_type=jnp.float32,
        )

    grams = []
    for k in range(1, n_st):
        gram_out[k] = gram_rows(peer(k))
        grams.append(send(gram_out.at[k], gram_in.at[k], gram_send.at[k], gram_recv.at[k],
                          {"st": peer(k)}))
    total = gram_rows(q)
    for k in range(1, n_st):
        grams[k - 1].wait()
        total += gram_in[k]
    for j in range(n_dom):
        chunk_out[j] = total[j * rows:(j + 1) * rows]
    chunks = [
        send(chunk_out.at[along(j)], chunk_in.at[j], chunk_send.at[j], chunk_recv.at[j],
             {"dom": along(j)})
        for j in range(1, n_dom)
    ]
    rest = []
    for m in range(1, n_st - 1):
        rest += send_rest(m)
    mine = chunk_out[d]
    for j in range(1, n_dom):
        chunks[j - 1].wait()
        mine += chunk_in[j]
    gathered[q, d] = mine

    def spread(source, slot):
        return [
            send(gathered.at[q, source], gathered.at[q, source],
                 st_send.at[k, slot], st_recv.at[k, slot], {"st": peer(k)})
            for k in range(1, n_st)
        ]

    doms = [
        send(gathered.at[q, d], gathered.at[q, d], dom_send.at[j], dom_recv.at[j],
             {"dom": along(j)})
        for j in range(1, n_dom)
    ]
    sent = spread(d, 0)
    for j in range(1, n_dom):
        doms[j - 1].wait_recv()
        sent += spread(lax.rem(d + n_dom - j, n_dom), j)
    for copy in doms:
        copy.wait_send()
    for copy in sent:
        copy.wait()
    rest += send_rest(n_st - 1)
    for p in range(n_st):
        for j in range(n_dom):
            start = p * states + j * rows
            gram_ref[start:start + rows, :] = gathered[p, j]

    gram = gram_ref[...]
    scale_sum = jnp.sqrt(jnp.sum(gram * gram, keepdims=True)) + epsilon

    def factor_of(product_rows, start):
        shape = product_rows.shape
        row_ids = start + lax.broadcasted_iota(jnp.int32, shape, 0)
        column_ids = lax.broadcasted_iota(jnp.int32, shape, 1)
        return jnp.where(row_ids == column_ids, 1.5, 0.0) - 0.5 * product_rows

    growing_ref[...] = gram / scale_sum
    for iteration in range(ROOT_ITERS - 1):
        if iteration == 0:
            factor = factor_of(growing_ref[...], 0)
            inverse = factor
        else:
            factor = factor_of(product(inverse_ref[...], growing_ref[...]), 0)
            inverse = product(factor, inverse_ref[...])
        growing_ref[...] = product(growing_ref[...], factor)
        inverse_ref[...] = inverse
    factor = factor_of(product(inverse_ref[band(q), :], growing_ref[...]), q * states)
    inverse = product(factor, inverse_ref[...])
    rotation = (inverse * jnp.sqrt(node_total / scale_sum)).astype(jnp.bfloat16)
    for copy in rest:
        copy.wait()
    for start in range(0, nodes, part):
        out_ref[:, start:start + part] = jnp.dot(
            rotation, full[:, start:start + part], preferred_element_type=jnp.float32
        ).astype(jnp.bfloat16)


def run_kernel(
    with_tail, orbitals, cell_matrix, connectivity, surface_nodes, cell_scale, potential
):
    states, nodes = orbitals.shape
    cells, node_cell = connectivity.shape
    surf = surface_nodes.shape[1]
    vmem = pl.BlockSpec(memory_space=pltpu.VMEM)
    smem = pl.BlockSpec(memory_space=pltpu.SMEM)
    hbm = pl.BlockSpec(memory_space=pl.ANY)
    bf16, f32 = jnp.bfloat16, jnp.float32
    n_dom, n_st = lax.axis_size("dom"), lax.axis_size("st")
    tail_scratch = []
    if with_tail:
        rows, states_all = states // n_dom, states * n_st
        square = pltpu.VMEM((states_all, states_all), f32)
        tail_scratch = [
            pltpu.VMEM((states_all, nodes), bf16),
            pltpu.VMEM((n_st, states, states_all), f32),
            pltpu.VMEM((n_st, states, states_all), f32),
            pltpu.VMEM((n_dom, rows, states_all), f32),
            pltpu.VMEM((n_dom, rows, states_all), f32),
            pltpu.VMEM((n_st, n_dom, rows, states_all), f32),
            square, square, square,
        ]
        tail_scratch += [pltpu.SemaphoreType.DMA((n_st,))] * 4
        tail_scratch += [pltpu.SemaphoreType.DMA((n_dom,))] * 4
        tail_scratch += [pltpu.SemaphoreType.DMA((n_st, n_dom))] * 2
        tail_scratch += [pltpu.SemaphoreType.DMA((n_st, n_st))] * 2
    return pl.pallas_call(
        functools.partial(kernel, n_dom, n_st, cells - cells // 4, with_tail),
        out_shape=jax.ShapeDtypeStruct((states, nodes), bf16),
        in_specs=[hbm, hbm, hbm, hbm, smem, hbm],
        out_specs=vmem,
        scratch_shapes=[
            pltpu.VMEM((node_cell, node_cell), bf16),
            pltpu.VMEM((cells, node_cell), jnp.int32),
            pltpu.VMEM((1, surf), jnp.int32),
            pltpu.VMEM((1, nodes), f32),
            pltpu.VMEM((states, nodes + surf), bf16),
            pltpu.VMEM((states, nodes), bf16),
            pltpu.VMEM((states, nodes + surf), f32),
            pltpu.VMEM((cells * node_cell, nodes + surf), bf16),
            pltpu.VMEM((nodes, surf), bf16),
            pltpu.VMEM((2 * states, cells * node_cell), bf16),
            pltpu.VMEM((DEGREE, states, surf), bf16),
            pltpu.VMEM((DEGREE, states, surf), bf16),
            pltpu.VMEM((DEGREE, states, surf), f32),
            pltpu.VMEM((DEGREE, states, surf), f32),
        ] + [pltpu.SemaphoreType.DMA((DEGREE,))] * 4 + [pltpu.SemaphoreType.DMA((5,))]
        + tail_scratch,
        compiler_params=pltpu.CompilerParams(
            collective_id=0, has_side_effects=True, vmem_limit_bytes=60 * 1024 * 1024
        ),
        name="filter_and_rotation" if with_tail else "filter",
    )(orbitals, cell_matrix, connectivity, surface_nodes, cell_scale, potential[None, :])


def newton_root(gram):
    highest = lax.Precision.HIGHEST
    states_all = gram.shape[0]
    scale_sum = jnp.sqrt(jnp.sum(gram * gram)) + epsilon
    identity = jnp.eye(states_all, dtype=jnp.float32)
    growing = gram / scale_sum
    inverse = identity
    for iteration in range(ROOT_ITERS):
        factor = 1.5 * identity - 0.5 * jnp.dot(inverse, growing, precision=highest)
        growing = jnp.dot(growing, factor, precision=highest)
        inverse = jnp.dot(factor, inverse, precision=highest)
    return (inverse, scale_sum)


def tail_in_parts(newest):
    slabs = lax.all_to_all(newest, "st", split_axis=1, concat_axis=0, tiled=True)
    gram_part = jnp.dot(slabs, slabs.T, preferred_element_type=jnp.float32)
    row_block = lax.psum_scatter(gram_part, "st", scatter_dimension=0, tiled=True)
    row_block = lax.psum(row_block, "dom")
    gram = lax.all_gather(row_block, "st", axis=0, tiled=True)
    inverse, scale_sum = newton_root(gram)
    node_total = lax.axis_size("dom") * newest.shape[1]
    rotation = (inverse * jnp.sqrt(node_total / scale_sum)).astype(jnp.bfloat16)
    rotated = jnp.dot(rotation.T, slabs, preferred_element_type=jnp.float32).astype(jnp.bfloat16)
    return lax.all_to_all(rotated, "st", split_axis=0, concat_axis=1, tiled=True)


def body(orbitals, *others):
    if orbitals.shape[0] % lax.axis_size("dom") == 0:
        return run_kernel(True, orbitals, *others)
    return tail_in_parts(run_kernel(False, orbitals, *others))


def solution(mesh):
    return jax.shard_map(
        body,
        mesh=mesh,
        in_specs=(P("st", "dom"), P(), P("dom", None), P("dom", None), P("dom"), P("dom")),
        out_specs=P("st", "dom"),
        check_vma=False,
    )
```

```python
import functools

import jax
import jax.numpy as jnp
from jax import lax
from jax.experimental import pallas as pl
from jax.experimental.pallas import tpu as pltpu
from jax.sharding import PartitionSpec as P

DEGREE = 3
ROOT_ITERS = 4
TILE = 256
MESH = pl.DeviceIdType.MESH

center = 7.0
half_width = 6.0
epsilon = 1e-06

NT = (((1,), (1,)), ((), ()))


def halves(values):
    high = values.astype(jnp.bfloat16)
    low = (values - high.astype(jnp.float32)).astype(jnp.bfloat16)
    return jnp.concatenate([high, low], axis=0)


def greet(n_dom, n_st, everyone):
    d, q = lax.axis_index("dom"), lax.axis_index("st")
    barrier = pltpu.get_barrier_semaphore()
    steps = range(1, n_dom) if everyone else (1, n_dom - 1)
    for j in steps:
        pl.semaphore_signal(
            barrier, inc=1, device_id={"dom": lax.rem(d + j, n_dom)}, device_id_type=MESH
        )
    if everyone:
        for k in range(1, n_st):
            pl.semaphore_signal(
                barrier, inc=1, device_id={"st": lax.rem(q + k, n_st)}, device_id_type=MESH
            )
    return barrier, len(steps) + (n_st - 1 if everyone else 0)


def kernel(
    n_dom, n_st, inner, with_tail,
    f_hbm, matrix_hbm, conn_hbm, surface_hbm, scale_ref, potential_hbm, out_ref,
    matrix_ref, conn_ref, surface_ref, potential_ref, flat, extended, history, totals, picks, picks_down,
    surface_pick, surface_down, masked, edge_out, edge_in, back_out, back_in,
    edge_send, edge_recv, back_send, back_recv, load_sems, *tail_refs,
):
    states, nodes = f_hbm.shape
    surf = surface_ref.shape[1]
    cells, node_cell = conn_ref.shape
    width = nodes + surf
    tile = TILE
    me = lax.axis_index("dom")
    after, before = lax.rem(me + 1, n_dom), lax.rem(me + n_dom - 1, n_dom)

    barrier, greetings = greet(n_dom, n_st, with_tail)
    loads = [
        pltpu.make_async_copy(src, dst, load_sems.at[index])
        for index, (src, dst) in enumerate([
            (conn_hbm, conn_ref), (surface_hbm, surface_ref),
            (f_hbm, flat), (matrix_hbm, matrix_ref),
            (potential_hbm, potential_ref),
        ])
    ]
    for load in loads:
        load.start()

    own_tiles, all_tiles = nodes // tile, width // tile
    one, zero = jnp.bfloat16(1), jnp.bfloat16(0)

    def places(ids):
        return jnp.bitwise_and(ids, tile - 1)

    def tiles_of(ids):
        return jnp.right_shift(ids, 8)

    def across(ids):
        shape = (tile, ids.shape[1])
        place = lax.broadcasted_iota(jnp.int32, shape, 0).astype(jnp.bfloat16)
        wanted = jnp.broadcast_to(places(ids).astype(jnp.bfloat16), shape)
        return jnp.where(place == wanted, one, zero)

    def downwards(column):
        shape = (column.shape[0], tile)
        place = lax.broadcasted_iota(jnp.int32, shape, 1).astype(jnp.bfloat16)
        wanted = jnp.broadcast_to(column, shape).astype(jnp.bfloat16)
        return jnp.where(place == wanted, one, zero)

    def gather(pick, ids, count):
        found_all = jnp.dot(
            extended[:count * states, :], pick, preferred_element_type=jnp.float32
        )
        place = jnp.broadcast_to(tiles_of(ids), (states, ids.shape[1]))
        found = found_all[:states]
        for t in range(1, count):
            found = jnp.where(place == t, found_all[t * states:(t + 1) * states], found)
        return found.astype(jnp.bfloat16)

    def scatter(values, pick_down, ids, count, slot):
        parts = halves(values)
        lanes = pl.ds(slot * node_cell, ids.shape[1])
        place = jnp.broadcast_to(tiles_of(ids).astype(jnp.bfloat16), parts.shape)
        for t in range(count):
            masked[pl.ds(t * 2 * states, 2 * states), lanes] = jnp.where(
                place == jnp.bfloat16(t), parts, jnp.zeros_like(parts)
            )
        spread = jnp.dot(
            masked[:count * 2 * states, lanes], pick_down, preferred_element_type=jnp.float32
        )
        for t in range(count):
            low = t * 2 * states
            totals[pl.ds(t * states, states), :] += (
                spread[low:low + states] + spread[low + states:low + 2 * states]
            )

    loads[0].wait()
    places_down = jnp.transpose(places(conn_ref[...]).astype(jnp.float32))
    for cell in range(cells):
        picks[cell] = across(conn_ref[pl.ds(cell, 1), :])
        picks_down[cell] = downwards(places_down[:, cell:cell + 1])
    for load in loads[1:]:
        load.wait()
    surface_ids = surface_ref[...]
    surface_pick[...] = across(surface_ids)
    surface_down[...] = jnp.transpose(surface_pick[...].astype(jnp.float32)).astype(jnp.bfloat16)
    for t in range(own_tiles):
        extended[pl.ds(t * states, states), :] = flat[:, t * tile:(t + 1) * tile]

    def run_cells(first, last, count):
        gathered = [
            gather(picks[cell], conn_ref[pl.ds(cell, 1), :], count) for cell in range(first, last)
        ]
        products = jnp.dot(
            jnp.concatenate(gathered, axis=0), matrix_ref[...], preferred_element_type=jnp.float32
        )
        for index in range(last - first):
            cell = first + index
            scaled = products[index * states:(index + 1) * states] * scale_ref[cell]
            scatter(scaled, picks_down[cell], conn_ref[pl.ds(cell, 1), :], count, index)

    pl.semaphore_wait(barrier, greetings)

    def one_step(step, carry):
        edge_out[step] = gather(surface_pick[...], surface_ids, own_tiles)
        edge = pltpu.make_async_remote_copy(
            src_ref=edge_out.at[step], dst_ref=edge_in.at[step],
            send_sem=edge_send.at[step], recv_sem=edge_recv.at[step],
            device_id={"dom": before}, device_id_type=MESH,
        )
        edge.start()
        totals[...] = jnp.zeros_like(totals)
        run_cells(0, inner // 2, own_tiles)
        edge.wait()
        for t in range(own_tiles, all_tiles):
            ghosts = edge_in[step, :, (t - own_tiles) * tile:(t - own_tiles + 1) * tile]
            extended[pl.ds(t * states, states), :] = jnp.where(
                me == n_dom - 1, jnp.zeros_like(ghosts), ghosts
            )
        run_cells(inner, cells, all_tiles)
        for t in range(own_tiles, all_tiles):
            back_out[step, :, (t - own_tiles) * tile:(t - own_tiles + 1) * tile] = (
                totals[pl.ds(t * states, states), :]
            )
        back = pltpu.make_async_remote_copy(
            src_ref=back_out.at[step], dst_ref=back_in.at[step],
            send_sem=back_send.at[step], recv_sem=back_recv.at[step],
            device_id={"dom": after}, device_id_type=MESH,
        )
        back.start()
        run_cells(inner // 2, inner, own_tiles)
        back.wait()
        returned = back_in[step]
        returned = jnp.where(me == 0, jnp.zeros_like(returned), returned)
        scatter(returned, surface_down[...], surface_ids, own_tiles, 0)
        first = step == 0
        for t in range(own_tiles):
            rows = pl.ds(t * states, states)
            old = extended[rows, :]
            newest = old.astype(jnp.float32)
            image = totals[rows, :] + potential_ref[:, t * tile:(t + 1) * tile] * newest
            shifted = (image - center * newest) / half_width
            later = 2.0 * shifted - history[rows, :].astype(jnp.float32)
            fresh = jnp.where(first, shifted, later).astype(jnp.bfloat16)
            history[rows, :] = old
            extended[rows, :] = fresh
        return carry

    history[...] = jnp.zeros_like(history)
    lax.fori_loop(0, DEGREE, one_step, 0)
    for t in range(own_tiles):
        flat[:, t * tile:(t + 1) * tile] = extended[pl.ds(t * states, states), :]
    if with_tail:
        tail_part(n_dom, n_st, float(n_dom * nodes), states, nodes, flat, out_ref, *tail_refs)
    else:
        out_ref[...] = flat[...]


def product(left, right):
    left_high = left.astype(jnp.bfloat16)
    left_low = (left - left_high.astype(jnp.float32)).astype(jnp.bfloat16)
    right_high = right.astype(jnp.bfloat16)
    right_low = (right - right_high.astype(jnp.float32)).astype(jnp.bfloat16)
    dot = functools.partial(jnp.dot, preferred_element_type=jnp.float32)
    return dot(left_high, right_high) + (dot(left_high, right_low) + dot(left_low, right_high))


def tail_part(
    n_dom, n_st, node_total, states, nodes,
    f_ref, out_ref,
    full, gram_out, gram_in, chunk_out, chunk_in, gathered, gram_ref, growing_ref, inverse_ref,
    *sems,
):
    (slab_send, slab_recv, gram_send, gram_recv, chunk_send, chunk_recv,
     dom_send, dom_recv, st_send, st_recv, rest_send, rest_recv) = sems
    part = nodes // n_st
    rows = states // n_dom
    states_all = states * n_st
    d, q = lax.axis_index("dom"), lax.axis_index("st")

    def peer(k):
        return lax.rem(q + k, n_st)

    def along(j):
        return lax.rem(d + j, n_dom)

    def send(src, dst, send_sem, recv_sem, target):
        copy = pltpu.make_async_remote_copy(
            src_ref=src, dst_ref=dst, send_sem=send_sem, recv_sem=recv_sem,
            device_id=target, device_id_type=MESH,
        )
        copy.start()
        return copy

    def columns(p):
        return pl.ds(pl.multiple_of(p * part, part), part)

    def band(p):
        return pl.ds(pl.multiple_of(p * states, states), states)

    slab = [
        send(f_ref.at[:, columns(peer(k))], full.at[band(q), columns(peer(k))],
             slab_send.at[k], slab_recv.at[k], {"st": peer(k)})
        for k in range(1, n_st)
    ]

    def send_rest(m):
        return [
            send(f_ref.at[:, columns(peer(k + m))], full.at[band(q), columns(peer(k + m))],
                 rest_send.at[k, m], rest_recv.at[k, m], {"st": peer(k)})
            for k in range(1, n_st)
        ]

    full[band(q), :] = f_ref[...]
    for copy in slab:
        copy.wait()

    def gram_rows(p):
        return lax.dot_general(
            full[band(p), columns(q)], full[:, columns(q)], NT,
            preferred_element_type=jnp.float32,
        )

    grams = []
    for k in range(1, n_st):
        gram_out[k] = gram_rows(peer(k))
        grams.append(send(gram_out.at[k], gram_in.at[k], gram_send.at[k], gram_recv.at[k],
                          {"st": peer(k)}))
    total = gram_rows(q)
    for k in range(1, n_st):
        grams[k - 1].wait()
        total += gram_in[k]
    for j in range(n_dom):
        chunk_out[j] = total[j * rows:(j + 1) * rows]
    chunks = [
        send(chunk_out.at[along(j)], chunk_in.at[j], chunk_send.at[j], chunk_recv.at[j],
             {"dom": along(j)})
        for j in range(1, n_dom)
    ]
    rest = []
    for m in range(1, n_st - 1):
        rest += send_rest(m)
    mine = chunk_out[d]
    for j in range(1, n_dom):
        chunks[j - 1].wait()
        mine += chunk_in[j]
    gathered[q, d] = mine

    def spread(source, slot):
        return [
            send(gathered.at[q, source], gathered.at[q, source],
                 st_send.at[k, slot], st_recv.at[k, slot], {"st": peer(k)})
            for k in range(1, n_st)
        ]

    doms = [
        send(gathered.at[q, d], gathered.at[q, d], dom_send.at[j], dom_recv.at[j],
             {"dom": along(j)})
        for j in range(1, n_dom)
    ]
    sent = spread(d, 0)
    for j in range(1, n_dom):
        doms[j - 1].wait_recv()
        sent += spread(lax.rem(d + n_dom - j, n_dom), j)
    for copy in doms:
        copy.wait_send()
    for copy in sent:
        copy.wait()
    rest += send_rest(n_st - 1)
    for p in range(n_st):
        for j in range(n_dom):
            start = p * states + j * rows
            gram_ref[start:start + rows, :] = gathered[p, j]

    gram = gram_ref[...]
    scale_sum = jnp.sqrt(jnp.sum(gram * gram, keepdims=True)) + epsilon

    def factor_of(product_rows, start):
        shape = product_rows.shape
        row_ids = start + lax.broadcasted_iota(jnp.int32, shape, 0)
        column_ids = lax.broadcasted_iota(jnp.int32, shape, 1)
        return jnp.where(row_ids == column_ids, 1.5, 0.0) - 0.5 * product_rows

    growing_ref[...] = gram / scale_sum
    for iteration in range(ROOT_ITERS - 1):
        if iteration == 0:
            factor = factor_of(growing_ref[...], 0)
            inverse = factor
        else:
            factor = factor_of(product(inverse_ref[...], growing_ref[...]), 0)
            inverse = product(factor, inverse_ref[...])
        growing_ref[...] = product(growing_ref[...], factor)
        inverse_ref[...] = inverse
    factor = factor_of(product(inverse_ref[band(q), :], growing_ref[...]), q * states)
    inverse = product(factor, inverse_ref[...])
    rotation = (inverse * jnp.sqrt(node_total / scale_sum)).astype(jnp.bfloat16)
    for copy in rest:
        copy.wait()
    for start in range(0, nodes, part):
        out_ref[:, start:start + part] = jnp.dot(
            rotation, full[:, start:start + part], preferred_element_type=jnp.float32
        ).astype(jnp.bfloat16)


def run_kernel(
    with_tail, orbitals, cell_matrix, connectivity, surface_nodes, cell_scale, potential
):
    states, nodes = orbitals.shape
    cells, node_cell = connectivity.shape
    surf = surface_nodes.shape[1]
    vmem = pl.BlockSpec(memory_space=pltpu.VMEM)
    smem = pl.BlockSpec(memory_space=pltpu.SMEM)
    hbm = pl.BlockSpec(memory_space=pl.ANY)
    bf16, f32 = jnp.bfloat16, jnp.float32
    n_dom, n_st = lax.axis_size("dom"), lax.axis_size("st")
    tail_scratch = []
    if with_tail:
        rows, states_all = states // n_dom, states * n_st
        square = pltpu.VMEM((states_all, states_all), f32)
        tail_scratch = [
            pltpu.VMEM((states_all, nodes), bf16),
            pltpu.VMEM((n_st, states, states_all), f32),
            pltpu.VMEM((n_st, states, states_all), f32),
            pltpu.VMEM((n_dom, rows, states_all), f32),
            pltpu.VMEM((n_dom, rows, states_all), f32),
            pltpu.VMEM((n_st, n_dom, rows, states_all), f32),
            square, square, square,
        ]
        tail_scratch += [pltpu.SemaphoreType.DMA((n_st,))] * 4
        tail_scratch += [pltpu.SemaphoreType.DMA((n_dom,))] * 4
        tail_scratch += [pltpu.SemaphoreType.DMA((n_st, n_dom))] * 2
        tail_scratch += [pltpu.SemaphoreType.DMA((n_st, n_st))] * 2
    return pl.pallas_call(
        functools.partial(kernel, n_dom, n_st, cells - cells // 4, with_tail),
        out_shape=jax.ShapeDtypeStruct((states, nodes), bf16),
        in_specs=[hbm, hbm, hbm, hbm, smem, hbm],
        out_specs=vmem,
        scratch_shapes=[
            pltpu.VMEM((node_cell, node_cell), bf16),
            pltpu.VMEM((cells, node_cell), jnp.int32),
            pltpu.VMEM((1, surf), jnp.int32),
            pltpu.VMEM((1, nodes), f32),
            pltpu.VMEM((states, nodes), bf16),
            pltpu.VMEM(((nodes + surf) // TILE * states, TILE), bf16),
            pltpu.VMEM((nodes // TILE * states, TILE), bf16),
            pltpu.VMEM(((nodes + surf) // TILE * states, TILE), f32),
            pltpu.VMEM((cells, TILE, node_cell), bf16),
            pltpu.VMEM((cells, node_cell, TILE), bf16),
            pltpu.VMEM((TILE, surf), bf16),
            pltpu.VMEM((surf, TILE), bf16),
            pltpu.VMEM(((nodes + surf) // TILE * 2 * states, cells * node_cell // 2), bf16),
            pltpu.VMEM((DEGREE, states, surf), bf16),
            pltpu.VMEM((DEGREE, states, surf), bf16),
            pltpu.VMEM((DEGREE, states, surf), f32),
            pltpu.VMEM((DEGREE, states, surf), f32),
        ] + [pltpu.SemaphoreType.DMA((DEGREE,))] * 4 + [pltpu.SemaphoreType.DMA((5,))]
        + tail_scratch,
        compiler_params=pltpu.CompilerParams(
            collective_id=0, has_side_effects=True, vmem_limit_bytes=60 * 1024 * 1024
        ),
        name="filter_and_rotation" if with_tail else "filter",
    )(orbitals, cell_matrix, connectivity, surface_nodes, cell_scale, potential[None, :])


def newton_root(gram):
    highest = lax.Precision.HIGHEST
    states_all = gram.shape[0]
    scale_sum = jnp.sqrt(jnp.sum(gram * gram)) + epsilon
    identity = jnp.eye(states_all, dtype=jnp.float32)
    growing = gram / scale_sum
    inverse = identity
    for iteration in range(ROOT_ITERS):
        factor = 1.5 * identity - 0.5 * jnp.dot(inverse, growing, precision=highest)
        growing = jnp.dot(growing, factor, precision=highest)
        inverse = jnp.dot(factor, inverse, precision=highest)
    return (inverse, scale_sum)


def tail_in_parts(newest):
    slabs = lax.all_to_all(newest, "st", split_axis=1, concat_axis=0, tiled=True)
    gram_part = jnp.dot(slabs, slabs.T, preferred_element_type=jnp.float32)
    row_block = lax.psum_scatter(gram_part, "st", scatter_dimension=0, tiled=True)
    row_block = lax.psum(row_block, "dom")
    gram = lax.all_gather(row_block, "st", axis=0, tiled=True)
    inverse, scale_sum = newton_root(gram)
    node_total = lax.axis_size("dom") * newest.shape[1]
    rotation = (inverse * jnp.sqrt(node_total / scale_sum)).astype(jnp.bfloat16)
    rotated = jnp.dot(rotation.T, slabs, preferred_element_type=jnp.float32).astype(jnp.bfloat16)
    return lax.all_to_all(rotated, "st", split_axis=0, concat_axis=1, tiled=True)


def body(orbitals, *others):
    if orbitals.shape[0] % lax.axis_size("dom") == 0:
        return run_kernel(True, orbitals, *others)
    return tail_in_parts(run_kernel(False, orbitals, *others))


def solution(mesh):
    return jax.shard_map(
        body,
        mesh=mesh,
        in_specs=(P("st", "dom"), P(), P("dom", None), P("dom", None), P("dom"), P("dom")),
        out_specs=P("st", "dom"),
        check_vma=False,
    )
```

```python
import functools

import jax
import jax.numpy as jnp
from jax import lax
from jax.experimental import pallas as pl
from jax.experimental.pallas import tpu as pltpu
from jax.sharding import PartitionSpec as P

DEGREE = 3
ROOT_ITERS = 4
TILE = 256
MESH = pl.DeviceIdType.MESH

center = 7.0
half_width = 6.0
epsilon = 1e-06

NT = (((1,), (1,)), ((), ()))


def halves(values):
    high = values.astype(jnp.bfloat16)
    low = (values - high.astype(jnp.float32)).astype(jnp.bfloat16)
    return jnp.concatenate([high, low], axis=0)


def greet(n_dom, n_st, everyone):
    d, q = lax.axis_index("dom"), lax.axis_index("st")
    barrier = pltpu.get_barrier_semaphore()
    steps = range(1, n_dom) if everyone else (1, n_dom - 1)
    for j in steps:
        pl.semaphore_signal(
            barrier, inc=1, device_id={"dom": lax.rem(d + j, n_dom)}, device_id_type=MESH
        )
    if everyone:
        for k in range(1, n_st):
            pl.semaphore_signal(
                barrier, inc=1, device_id={"st": lax.rem(q + k, n_st)}, device_id_type=MESH
            )
    return barrier, len(steps) + (n_st - 1 if everyone else 0)


def kernel(
    n_dom, n_st, inner, with_tail,
    f_hbm, matrix_hbm, conn_hbm, surface_hbm, scale_ref, potential_hbm, out_ref,
    matrix_ref, conn_ref, surface_ref, potential_ref, flat, extended, history, totals, picks, picks_down,
    surface_pick, surface_down, pair, edge_out, edge_in, back_out, back_in,
    edge_send, edge_recv, back_send, back_recv, load_sems, *tail_refs,
):
    states, nodes = f_hbm.shape
    surf = surface_ref.shape[1]
    cells, node_cell = conn_ref.shape
    width = nodes + surf
    tile = TILE
    me = lax.axis_index("dom")
    after, before = lax.rem(me + 1, n_dom), lax.rem(me + n_dom - 1, n_dom)

    barrier, greetings = greet(n_dom, n_st, with_tail)
    loads = [
        pltpu.make_async_copy(src, dst, load_sems.at[index])
        for index, (src, dst) in enumerate([
            (conn_hbm, conn_ref), (surface_hbm, surface_ref),
            (f_hbm, flat), (matrix_hbm, matrix_ref),
            (potential_hbm, potential_ref),
        ])
    ]
    for load in loads:
        load.start()

    own_tiles, all_tiles = nodes // tile, width // tile
    one, zero = jnp.bfloat16(1), jnp.bfloat16(0)

    def places(ids):
        return jnp.bitwise_and(ids, tile - 1)

    def tiles_of(ids):
        return jnp.right_shift(ids, 8)

    def across(ids):
        shape = (tile, ids.shape[1])
        place = lax.broadcasted_iota(jnp.int32, shape, 0).astype(jnp.bfloat16)
        wanted = jnp.broadcast_to(places(ids).astype(jnp.bfloat16), shape)
        return jnp.where(place == wanted, one, zero)

    def build_down(target, first, column, count):
        shape = (column.shape[0], tile)
        place = lax.broadcasted_iota(jnp.int32, shape, 1).astype(jnp.bfloat16)
        wanted = jnp.broadcast_to(column, shape)
        rows = pl.ds(first, column.shape[0])

        def build_tile(index, carry):
            start = index * tile
            shifted = (wanted - start.astype(jnp.float32)).astype(jnp.bfloat16)
            target[rows, pl.ds(pl.multiple_of(start, tile), tile)] = jnp.where(
                place == shifted, one, zero
            )
            return carry

        lax.fori_loop(0, count, build_tile, 0)

    def gather(pick, ids, count):
        found_all = jnp.dot(
            extended[:count * states, :], pick, preferred_element_type=jnp.float32
        )
        place = jnp.broadcast_to(tiles_of(ids), (states, ids.shape[1]))
        found = found_all[:states]
        for t in range(1, count):
            found = jnp.where(place == t, found_all[t * states:(t + 1) * states], found)
        return found.astype(jnp.bfloat16)

    loads[0].wait()
    ids_down = jnp.transpose(conn_ref[...].astype(jnp.float32))
    for cell in range(cells):
        picks[cell] = across(conn_ref[pl.ds(cell, 1), :])
        build_down(
            picks_down, cell * node_cell, ids_down[:, cell:cell + 1],
            own_tiles if cell < inner else all_tiles,
        )
    for load in loads[1:]:
        load.wait()
    surface_ids = surface_ref[...]
    surface_pick[...] = across(surface_ids)
    surface_column = jnp.transpose(
        jnp.broadcast_to(surface_ids.astype(jnp.float32), (8, surf))
    )[:, :1]
    build_down(surface_down, 0, surface_column, own_tiles)
    for t in range(own_tiles):
        extended[pl.ds(t * states, states), :] = flat[:, t * tile:(t + 1) * tile]

    def run_cells(first, last, count):
        gathered = [
            gather(picks[cell], conn_ref[pl.ds(cell, 1), :], count) for cell in range(first, last)
        ]
        products = jnp.dot(
            jnp.concatenate(gathered, axis=0), matrix_ref[...], preferred_element_type=jnp.float32
        )
        for index in range(last - first):
            cell = first + index
            scaled = products[index * states:(index + 1) * states] * scale_ref[cell]
            pair[:, index * node_cell:(index + 1) * node_cell] = halves(scaled)
        lanes = (last - first) * node_cell
        group = pl.ds(first * node_cell, lanes)
        for t in range(count):
            columns = pl.ds(t * tile, tile)
            spread = jnp.dot(
                pair[:, :lanes], picks_down[group, columns], preferred_element_type=jnp.float32
            )
            totals[:, columns] += spread[:states] + spread[states:]

    pl.semaphore_wait(barrier, greetings)

    def one_step(step, carry):
        edge_out[step] = gather(surface_pick[...], surface_ids, own_tiles)
        edge = pltpu.make_async_remote_copy(
            src_ref=edge_out.at[step], dst_ref=edge_in.at[step],
            send_sem=edge_send.at[step], recv_sem=edge_recv.at[step],
            device_id={"dom": before}, device_id_type=MESH,
        )
        edge.start()
        totals[...] = jnp.zeros_like(totals)
        run_cells(0, inner // 2, own_tiles)
        edge.wait()
        for t in range(own_tiles, all_tiles):
            ghosts = edge_in[step, :, (t - own_tiles) * tile:(t - own_tiles + 1) * tile]
            extended[pl.ds(t * states, states), :] = jnp.where(
                me == n_dom - 1, jnp.zeros_like(ghosts), ghosts
            )
        run_cells(inner, cells, all_tiles)
        back_out[step] = totals[:, nodes:]
        back = pltpu.make_async_remote_copy(
            src_ref=back_out.at[step], dst_ref=back_in.at[step],
            send_sem=back_send.at[step], recv_sem=back_recv.at[step],
            device_id={"dom": after}, device_id_type=MESH,
        )
        back.start()
        run_cells(inner // 2, inner, own_tiles)
        back.wait()
        returned = back_in[step]
        returned = jnp.where(me == 0, jnp.zeros_like(returned), returned)
        parts = halves(returned)
        first = step == 0
        for t in range(own_tiles):
            rows = pl.ds(t * states, states)
            old = extended[rows, :]
            newest = old.astype(jnp.float32)
            columns = pl.ds(t * tile, tile)
            spread = jnp.dot(parts, surface_down[:, columns], preferred_element_type=jnp.float32)
            total = totals[:, columns] + (spread[:states] + spread[states:])
            image = total + potential_ref[:, columns] * newest
            shifted = (image - center * newest) / half_width
            later = 2.0 * shifted - history[rows, :].astype(jnp.float32)
            fresh = jnp.where(first, shifted, later).astype(jnp.bfloat16)
            history[rows, :] = old
            extended[rows, :] = fresh
        return carry

    history[...] = jnp.zeros_like(history)
    lax.fori_loop(0, DEGREE, one_step, 0)
    for t in range(own_tiles):
        flat[:, t * tile:(t + 1) * tile] = extended[pl.ds(t * states, states), :]
    if with_tail:
        tail_part(n_dom, n_st, float(n_dom * nodes), states, nodes, flat, out_ref, *tail_refs)
    else:
        out_ref[...] = flat[...]


def product(left, right):
    left_high = left.astype(jnp.bfloat16)
    left_low = (left - left_high.astype(jnp.float32)).astype(jnp.bfloat16)
    right_high = right.astype(jnp.bfloat16)
    right_low = (right - right_high.astype(jnp.float32)).astype(jnp.bfloat16)
    return jnp.dot(
        jnp.concatenate([left_high, left_high, left_low], axis=1),
        jnp.concatenate([right_high, right_low, right_high], axis=0),
        preferred_element_type=jnp.float32,
    )


def tail_part(
    n_dom, n_st, node_total, states, nodes,
    f_ref, out_ref,
    full, gram_out, gram_in, chunk_out, chunk_in, gathered, gram_ref, growing_ref, inverse_ref,
    *sems,
):
    (slab_send, slab_recv, gram_send, gram_recv, chunk_send, chunk_recv,
     dom_send, dom_recv, st_send, st_recv, rest_send, rest_recv) = sems
    part = nodes // n_st
    rows = states // n_dom
    states_all = states * n_st
    d, q = lax.axis_index("dom"), lax.axis_index("st")

    def peer(k):
        return lax.rem(q + k, n_st)

    def along(j):
        return lax.rem(d + j, n_dom)

    def send(src, dst, send_sem, recv_sem, target):
        copy = pltpu.make_async_remote_copy(
            src_ref=src, dst_ref=dst, send_sem=send_sem, recv_sem=recv_sem,
            device_id=target, device_id_type=MESH,
        )
        copy.start()
        return copy

    def columns(p):
        return pl.ds(pl.multiple_of(p * part, part), part)

    def band(p):
        return pl.ds(pl.multiple_of(p * states, states), states)

    slab = [
        send(f_ref.at[:, columns(peer(k))], full.at[band(q), columns(peer(k))],
             slab_send.at[k], slab_recv.at[k], {"st": peer(k)})
        for k in range(1, n_st)
    ]

    def send_rest(m):
        return [
            send(f_ref.at[:, columns(peer(k + m))], full.at[band(q), columns(peer(k + m))],
                 rest_send.at[k, m], rest_recv.at[k, m], {"st": peer(k)})
            for k in range(1, n_st)
        ]

    full[band(q), :] = f_ref[...]
    for copy in slab:
        copy.wait()

    def gram_rows(p):
        return lax.dot_general(
            full[band(p), columns(q)], full[:, columns(q)], NT,
            preferred_element_type=jnp.float32,
        )

    grams = []
    for k in range(1, n_st):
        gram_out[k] = gram_rows(peer(k))
        grams.append(send(gram_out.at[k], gram_in.at[k], gram_send.at[k], gram_recv.at[k],
                          {"st": peer(k)}))
    total = gram_rows(q)
    for k in range(1, n_st):
        grams[k - 1].wait()
        total += gram_in[k]
    for j in range(n_dom):
        chunk_out[j] = total[j * rows:(j + 1) * rows]
    chunks = [
        send(chunk_out.at[along(j)], chunk_in.at[j], chunk_send.at[j], chunk_recv.at[j],
             {"dom": along(j)})
        for j in range(1, n_dom)
    ]
    rest = []
    for m in range(1, n_st - 1):
        rest += send_rest(m)
    mine = chunk_out[d]
    for j in range(1, n_dom):
        chunks[j - 1].wait()
        mine += chunk_in[j]
    gathered[q, d] = mine

    def spread(source, slot):
        return [
            send(gathered.at[q, source], gathered.at[q, source],
                 st_send.at[k, slot], st_recv.at[k, slot], {"st": peer(k)})
            for k in range(1, n_st)
        ]

    doms = [
        send(gathered.at[q, d], gathered.at[q, d], dom_send.at[j], dom_recv.at[j],
             {"dom": along(j)})
        for j in range(1, n_dom)
    ]
    sent = spread(d, 0)
    for j in range(1, n_dom):
        doms[j - 1].wait_recv()
        sent += spread(lax.rem(d + n_dom - j, n_dom), j)
    for copy in doms:
        copy.wait_send()
    for copy in sent:
        copy.wait()
    rest += send_rest(n_st - 1)
    for p in range(n_st):
        for j in range(n_dom):
            start = p * states + j * rows
            gram_ref[start:start + rows, :] = gathered[p, j]

    gram = gram_ref[...]
    scale_sum = jnp.sqrt(jnp.sum(gram * gram, keepdims=True)) + epsilon

    def factor_of(product_rows, start):
        shape = product_rows.shape
        row_ids = start + lax.broadcasted_iota(jnp.int32, shape, 0)
        column_ids = lax.broadcasted_iota(jnp.int32, shape, 1)
        return jnp.where(row_ids == column_ids, 1.5, 0.0) - 0.5 * product_rows

    growing_ref[...] = gram / scale_sum
    for iteration in range(ROOT_ITERS - 1):
        if iteration == 0:
            factor = factor_of(growing_ref[...], 0)
            inverse = factor
        else:
            factor = factor_of(product(inverse_ref[...], growing_ref[...]), 0)
            inverse = product(factor, inverse_ref[...])
        growing_ref[...] = product(growing_ref[...], factor)
        inverse_ref[...] = inverse
    factor = factor_of(product(inverse_ref[band(q), :], growing_ref[...]), q * states)
    inverse = product(factor, inverse_ref[...])
    rotation = (inverse * jnp.sqrt(node_total / scale_sum)).astype(jnp.bfloat16)
    for copy in rest:
        copy.wait()
    for start in range(0, nodes, part):
        out_ref[:, start:start + part] = jnp.dot(
            rotation, full[:, start:start + part], preferred_element_type=jnp.float32
        ).astype(jnp.bfloat16)


def run_kernel(
    with_tail, orbitals, cell_matrix, connectivity, surface_nodes, cell_scale, potential
):
    states, nodes = orbitals.shape
    cells, node_cell = connectivity.shape
    surf = surface_nodes.shape[1]
    vmem = pl.BlockSpec(memory_space=pltpu.VMEM)
    smem = pl.BlockSpec(memory_space=pltpu.SMEM)
    hbm = pl.BlockSpec(memory_space=pl.ANY)
    bf16, f32 = jnp.bfloat16, jnp.float32
    n_dom, n_st = lax.axis_size("dom"), lax.axis_size("st")
    tail_scratch = []
    if with_tail:
        rows, states_all = states // n_dom, states * n_st
        square = pltpu.VMEM((states_all, states_all), f32)
        tail_scratch = [
            pltpu.VMEM((states_all, nodes), bf16),
            pltpu.VMEM((n_st, states, states_all), f32),
            pltpu.VMEM((n_st, states, states_all), f32),
            pltpu.VMEM((n_dom, rows, states_all), f32),
            pltpu.VMEM((n_dom, rows, states_all), f32),
            pltpu.VMEM((n_st, n_dom, rows, states_all), f32),
            square, square, square,
        ]
        tail_scratch += [pltpu.SemaphoreType.DMA((n_st,))] * 4
        tail_scratch += [pltpu.SemaphoreType.DMA((n_dom,))] * 4
        tail_scratch += [pltpu.SemaphoreType.DMA((n_st, n_dom))] * 2
        tail_scratch += [pltpu.SemaphoreType.DMA((n_st, n_st))] * 2
    return pl.pallas_call(
        functools.partial(kernel, n_dom, n_st, cells - cells // 4, with_tail),
        out_shape=jax.ShapeDtypeStruct((states, nodes), bf16),
        in_specs=[hbm, hbm, hbm, hbm, smem, hbm],
        out_specs=vmem,
        scratch_shapes=[
            pltpu.VMEM((node_cell, node_cell), bf16),
            pltpu.VMEM((cells, node_cell), jnp.int32),
            pltpu.VMEM((1, surf), jnp.int32),
            pltpu.VMEM((1, nodes), f32),
            pltpu.VMEM((states, nodes), bf16),
            pltpu.VMEM(((nodes + surf) // TILE * states, TILE), bf16),
            pltpu.VMEM((nodes // TILE * states, TILE), bf16),
            pltpu.VMEM((states, nodes + surf), f32),
            pltpu.VMEM((cells, TILE, node_cell), bf16),
            pltpu.VMEM((cells * node_cell, nodes + surf), bf16),
            pltpu.VMEM((TILE, surf), bf16),
            pltpu.VMEM((surf, nodes), bf16),
            pltpu.VMEM((2 * states, cells * node_cell // 2), bf16),
            pltpu.VMEM((DEGREE, states, surf), bf16),
            pltpu.VMEM((DEGREE, states, surf), bf16),
            pltpu.VMEM((DEGREE, states, surf), f32),
            pltpu.VMEM((DEGREE, states, surf), f32),
        ] + [pltpu.SemaphoreType.DMA((DEGREE,))] * 4 + [pltpu.SemaphoreType.DMA((5,))]
        + tail_scratch,
        compiler_params=pltpu.CompilerParams(
            collective_id=0, has_side_effects=True, vmem_limit_bytes=60 * 1024 * 1024
        ),
        name="filter_and_rotation" if with_tail else "filter",
    )(orbitals, cell_matrix, connectivity, surface_nodes, cell_scale, potential[None, :])


def newton_root(gram):
    highest = lax.Precision.HIGHEST
    states_all = gram.shape[0]
    scale_sum = jnp.sqrt(jnp.sum(gram * gram)) + epsilon
    identity = jnp.eye(states_all, dtype=jnp.float32)
    growing = gram / scale_sum
    inverse = identity
    for iteration in range(ROOT_ITERS):
        factor = 1.5 * identity - 0.5 * jnp.dot(inverse, growing, precision=highest)
        growing = jnp.dot(growing, factor, precision=highest)
        inverse = jnp.dot(factor, inverse, precision=highest)
    return (inverse, scale_sum)


def tail_in_parts(newest):
    slabs = lax.all_to_all(newest, "st", split_axis=1, concat_axis=0, tiled=True)
    gram_part = jnp.dot(slabs, slabs.T, preferred_element_type=jnp.float32)
    row_block = lax.psum_scatter(gram_part, "st", scatter_dimension=0, tiled=True)
    row_block = lax.psum(row_block, "dom")
    gram = lax.all_gather(row_block, "st", axis=0, tiled=True)
    inverse, scale_sum = newton_root(gram)
    node_total = lax.axis_size("dom") * newest.shape[1]
    rotation = (inverse * jnp.sqrt(node_total / scale_sum)).astype(jnp.bfloat16)
    rotated = jnp.dot(rotation.T, slabs, preferred_element_type=jnp.float32).astype(jnp.bfloat16)
    return lax.all_to_all(rotated, "st", split_axis=0, concat_axis=1, tiled=True)


def body(orbitals, *others):
    if orbitals.shape[0] % lax.axis_size("dom") == 0:
        return run_kernel(True, orbitals, *others)
    return tail_in_parts(run_kernel(False, orbitals, *others))


def solution(mesh):
    return jax.shard_map(
        body,
        mesh=mesh,
        in_specs=(P("st", "dom"), P(), P("dom", None), P("dom", None), P("dom"), P("dom")),
        out_specs=P("st", "dom"),
        check_vma=False,
    )
```
